256 devices in a mesh: seq: 64 (over z_lo, y, x, core), mp: 4 (over z_hi).
Axes of the slice: x: 4, y: 4, z: 8 (z_hi: 4, z_lo: 2; z = z_hi * 2 + z_lo), core: 2. Of those that a mesh axis runs over, the one named last changes fastest.
Arguments:
- byte_states: bfloat16 [32768, 1024], P('seq'), may hold values from -6 to 6
- byte_patch: int32 [64, 512], P('seq'), may hold values from 0 to 15, as said below
- pool_score: bfloat16 [1024, 16], P(None, 'mp'), may hold values from -1 to 1
- w_query: bfloat16 [1024, 2048], P(None, 'mp'), may hold values from -1 to 1
- w_key: bfloat16 [1024, 2048], P(None, 'mp'), may hold values from -1 to 1
- w_value: bfloat16 [1024, 2048], P(None, 'mp'), may hold values from -0.1875 to 0.1875
- out_grad: bfloat16 [1024, 2048], P('seq', 'mp'), may hold values from -6 to 6
Outputs:
- grad_bytes: bfloat16 [32768, 1024], P('seq')
- grad_query: float32 [1024, 2048], P('seq', 'mp')
- grad_key: float32 [1024, 2048], P('seq', 'mp')
- grad_value: float32 [1024, 2048], P('seq', 'mp')
- grad_score: float32 [1024, 16], P('seq', 'mp')
The draws below stay inside these ranges and needn't reach their ends.
Inputs may be any that keep to these rules, and one draw needn't show every extreme that they name: `byte_patch`: in each row the patch index starts at 0, never falls and rises by at most 1 from byte to byte; in some row it reaches 15.
All inputs are finite; a program needn't handle non-finite values.
Results may differ from the reference program's by a relative error of at most 0.03.
The reference program's roundings to bfloat16 on the way count: a program that leaves them out, or rounds other values in their place, can miss the bound.
Values may be sent and summed in bfloat16 or wider, within the bound.
A program may use at most 64 MiB of HBM per device.

```python
import jax
import jax.numpy as jnp
from jax import lax

DB = 1024
HEADS = 16
HD = 128
B_DEV = 512
PMAX = 16
DP = 2048
SHARDS = 64
BYTES = 32768
SLOTS = 1024
N_SEQ = 64


def patch_layout(key):
    key = jax.random.fold_in(key, 11)
    key_count, key_full, key_perm = jax.random.split(key, 3)
    counts = jax.random.randint(key_count, (SHARDS,), PMAX // 4, PMAX + 1)
    full = jax.random.randint(key_full, (), 0, SHARDS)
    counts = jnp.where(jnp.arange(SHARDS) == full, PMAX, counts)
    keys = jax.random.split(key_perm, SHARDS)
    perms = jax.vmap(lambda k: jax.random.permutation(k, B_DEV - 1))(keys)
    ranks = jnp.argsort(perms, axis=1).astype(jnp.int32)
    marks = (ranks < counts[:, None] - 1).astype(jnp.int32)
    marks = jnp.concatenate([jnp.zeros((SHARDS, 1), jnp.int32), marks], axis=1)
    return jnp.cumsum(marks, axis=1).astype(jnp.int32)


def draw_byte_patch(key, part):
    return patch_layout(key)


def draw_byte_states(key, part):
    key = jax.random.fold_in(key, 31)
    key_base = jax.random.fold_in(key, 0)
    states = jnp.clip(jax.random.normal(key_base, (SHARDS, B_DEV, DB), jnp.float32), -6.0, 6.0)
    return states.reshape(SHARDS * B_DEV, DB).astype(jnp.bfloat16)


def draw_pool_score(key, part):
    key = jax.random.fold_in(key, 41)
    key_jitter = jax.random.fold_in(key, 0)
    fan_scale = DB ** (-0.5)
    values = jnp.clip(jax.random.normal(key_jitter, (DB, HEADS), jnp.float32), -4.0, 4.0) * fan_scale
    return values.astype(jnp.bfloat16)


def draw_w_query(key, part):
    key = jax.random.fold_in(key, 51)
    fan_scale = DB ** (-0.5)
    weights = jnp.clip(jax.random.normal(key, (DB, DP), jnp.float32), -4.0, 4.0) * fan_scale
    return weights.astype(jnp.bfloat16)


def draw_w_key(key, part):
    key = jax.random.fold_in(key, 52)
    fan_scale = DB ** (-0.5)
    weights = jnp.clip(jax.random.normal(key, (DB, DP), jnp.float32), -4.0, 4.0) * fan_scale
    return weights.astype(jnp.bfloat16)


def shard_levels(own_key, shape, shards, low, largest):
    loudness, own = 1.0, jax.random.fold_in(own_key, 6)
    for axis_at, shards_of in shards:
        draws = jnp.exp(jax.random.uniform(jax.random.fold_in(own, axis_at), (shards_of,), jnp.float32, low / len(shards), largest / len(shards)))
        loudness = loudness * jnp.repeat(draws, shape[axis_at] // shards_of).reshape([-1 if axis == axis_at else 1 for axis in range(len(shape))])
    return loudness


def gaussian(stream_key, extent, scale, bound, cuts=(), kind=jnp.bfloat16):
    array = scale * jax.random.normal(stream_key, extent, jnp.float32)
    if cuts:
        array = array * shard_levels(stream_key, extent, cuts, -0.22, 0.18)
    return jnp.clip(array, -bound, bound).astype(kind)


def setup_inputs(seed: int = 0) -> dict:
    key_list = jax.random.split(jax.random.key(seed), 8)
    byte_states = draw_byte_states(jax.random.fold_in(key_list[7], 71), 0)
    byte_patch = draw_byte_patch(jax.random.fold_in(key_list[7], 71), 0)
    pool_score = draw_pool_score(jax.random.fold_in(key_list[7], 71), 0)
    w_query = draw_w_query(jax.random.fold_in(key_list[7], 71), 0)
    w_key = draw_w_key(jax.random.fold_in(key_list[7], 71), 0)
    w_value = gaussian(key_list[5], (DB, DP), DB ** -0.5, 0.1875, ((1, 4),))
    out_grad = gaussian(key_list[6], (SLOTS, DP), 1.0, 6.0, ((0, 64), (1, 4)))
    return dict(byte_states=byte_states, byte_patch=byte_patch, pool_score=pool_score, w_query=w_query, w_key=w_key, w_value=w_value, out_grad=out_grad)


def segment_softmax(scores, member):
    peak = jnp.max(jnp.where(member[:, :, None], scores[None, :, :], -1e30), axis=1)
    byte_peak = jnp.sum(jnp.where(member[:, :, None], peak[:, None, :], 0.0), axis=0)
    expd = jnp.exp(scores - byte_peak)
    total = jnp.sum(jnp.where(member[:, :, None], expd[None, :, :], 0.0), axis=1)
    byte_total = jnp.sum(jnp.where(member[:, :, None], total[:, None, :], 0.0), axis=0)
    return expd / byte_total


def patch_sum_back(values, member):
    total = jnp.sum(jnp.where(member[:, :, None], values[None, :, :], 0.0), axis=1)
    return jnp.sum(jnp.where(member[:, :, None], total[:, None, :], 0.0), axis=0)


def shard_forward(states, ids, pool_score, w_query, w_key, w_value):
    member = ids[None, :] == jnp.arange(PMAX, dtype=jnp.int32)[:, None]
    onehot = member.astype(jnp.float32)
    scores = jnp.dot(states, pool_score, preferred_element_type=jnp.float32)
    attn = segment_softmax(scores, member)
    spread = jnp.repeat(attn, HD, axis=1)
    outs = []
    for weight in (w_query, w_key, w_value):
        proj = jnp.dot(states, weight, preferred_element_type=jnp.float32)
        outs.append(jnp.dot(onehot, proj * spread, precision=lax.Precision.HIGHEST).astype(jnp.bfloat16))
    return outs[0], outs[1], outs[2]


def head_backward(items, valid):
    qh, kh, vh, gh = items
    scale = HD ** -0.5
    s = jnp.dot(qh, kh.T, preferred_element_type=jnp.float32) * scale
    pos = jnp.arange(SLOTS, dtype=jnp.int32)
    mask = (pos[None, :] <= pos[:, None]) & valid[None, :]
    peak = jnp.max(jnp.where(mask, s, -1e30), axis=1, keepdims=True)
    expd = jnp.where(mask, jnp.exp(s - peak), 0.0)
    prob = expd / jnp.sum(expd, axis=1, keepdims=True)
    pb = prob.astype(jnp.bfloat16)
    outv = jnp.dot(pb, vh, preferred_element_type=jnp.float32)
    delta = jnp.sum(gh.astype(jnp.float32) * outv, axis=1, keepdims=True)
    dprob = jnp.dot(gh, vh.T, preferred_element_type=jnp.float32)
    dscore = (prob * (dprob - delta) * scale).astype(jnp.bfloat16)
    dq = jnp.dot(dscore, kh, preferred_element_type=jnp.float32)
    dk = jnp.dot(dscore.T, qh, preferred_element_type=jnp.float32)
    dv = jnp.dot(pb.T, gh, preferred_element_type=jnp.float32)
    return dq, dk, dv


def reference(byte_states, byte_patch, pool_score, w_query, w_key, w_value, out_grad):
    states = byte_states.reshape(N_SEQ, B_DEV, DB)
    q, k, v = lax.map(lambda t: shard_forward(t[0], t[1], pool_score, w_query, w_key, w_value), (states, byte_patch))
    q = q.reshape(SLOTS, DP)
    k = k.reshape(SLOTS, DP)
    v = v.reshape(SLOTS, DP)
    counts = byte_patch[:, -1] + 1
    valid = (jnp.arange(PMAX, dtype=jnp.int32)[None, :] < counts[:, None]).reshape(SLOTS)
    g = jnp.where(valid[:, None], out_grad, jnp.zeros_like(out_grad))

    def heads_of(x):
        return x.reshape(SLOTS, HEADS, HD).transpose(1, 0, 2)

    dq, dk, dv = lax.map(lambda t: head_backward(t, valid), (heads_of(q), heads_of(k), heads_of(v), heads_of(g)))

    def back(x):
        return x.transpose(1, 0, 2).reshape(N_SEQ, PMAX, DP).astype(jnp.bfloat16)

    dq, dk, dv = back(dq), back(dk), back(dv)

    def step(carry, t):
        x, ids, gq_p, gk_p, gv_p = t
        member = ids[None, :] == jnp.arange(PMAX, dtype=jnp.int32)[:, None]
        onehot_t = member.astype(jnp.float32).T
        scores = jnp.dot(x, pool_score, preferred_element_type=jnp.float32)
        attn = segment_softmax(scores, member)
        spread = jnp.repeat(attn, HD, axis=1)
        dattn = jnp.zeros((B_DEV, DP), jnp.float32)
        dys = []
        for weight, grad_p in ((w_query, gq_p), (w_key, gk_p), (w_value, gv_p)):
            proj = jnp.dot(x, weight, preferred_element_type=jnp.float32)
            back_rows = jnp.dot(onehot_t, grad_p.astype(jnp.float32), precision=lax.Precision.HIGHEST)
            dys.append((spread * back_rows).astype(jnp.bfloat16))
            dattn = dattn + back_rows * proj
        dattn = jnp.sum(dattn.reshape(B_DEV, HEADS, HD), axis=2)
        dscore = (attn * (dattn - patch_sum_back(attn * dattn, member))).astype(jnp.bfloat16)
        grads = []
        for dy in dys + [dscore]:
            grads.append(lax.dot_general(x, dy, (((0,), (0,)), ((), ())), preferred_element_type=jnp.float32))
        dx = jnp.dot(dys[0], w_query.T, preferred_element_type=jnp.float32)
        dx = dx + jnp.dot(dys[1], w_key.T, preferred_element_type=jnp.float32)
        dx = dx + jnp.dot(dys[2], w_value.T, preferred_element_type=jnp.float32)
        dx = dx + jnp.dot(dscore, pool_score.T, preferred_element_type=jnp.float32)
        carry = tuple(c + gr for c, gr in zip(carry, grads))
        return carry, dx.astype(jnp.bfloat16)

    init = (jnp.zeros((DB, DP), jnp.float32), jnp.zeros((DB, DP), jnp.float32), jnp.zeros((DB, DP), jnp.float32), jnp.zeros((DB, HEADS), jnp.float32))
    sums, dxs = lax.scan(step, init, (states, byte_patch, dq, dk, dv))
    return dxs.reshape(BYTES, DB), sums[0], sums[1], sums[2], sums[3]
```

```python
import jax
import jax.numpy as jnp
from jax import lax
from jax.experimental import pallas as pl
from jax.experimental.pallas import tpu as pltpu
from jax.sharding import PartitionSpec as P

HD = 128
PM = 16
NH = 4
NM = 4
NS = 64
NE = 32
NC = 8
B = 512
DB = 1024
SLOTS = 1024
QB = 256
SCALE = HD**-0.5
LOG2E = 1.4426950408889634
NEG = -1e30
MARK = 2.0**100
F32 = jnp.float32
BF16 = jnp.bfloat16
MESH = pl.DeviceIdType.MESH


def dot(a, b, dims):
    return lax.dot_general(a, b, (dims, ((), ())), preferred_element_type=F32)


def nn(a, b):
    return dot(a, b, ((1,), (0,)))


def nt(a, b):
    return dot(a, b, ((1,), (1,)))


def tn(a, b):
    return dot(a, b, ((0,), (0,)))


def split(a):
    hi = a.astype(BF16)
    return hi, (a - hi.astype(F32)).astype(BF16)


def pool_softmax(scores, member):
    t = jnp.where(member, scores, NEG)
    peak = jnp.max(t, axis=1, keepdims=True)
    expd = jnp.where(member, jnp.exp(t - peak), 0.0)
    total = jnp.sum(expd, axis=1, keepdims=True)
    return expd / jnp.maximum(total, 1e-30)


def kernel(
    x_hbm, ids_ref, pool_ref, wq_hbm, wk_hbm, wv_hbm, g_ref,
    dx_ref, gq_ref, gk_ref, gv_ref, gs_ref,
    x_v, w_v, wcat, qs, xps, rq, rxp, rp, kc, bias, pt, dst, dqkv, us, ru, gsend, rg, sc_send, rs, a_all,
    in_sem, pool_send, pool_recv, q_send, q_recv, x_send, x_recv, f_send, f_recv, fx_send, fx_recv,
    u_send, u_recv, g_send, g_recv, s_send, s_recv,
):
    me = lax.axis_index("seq")
    m = lax.axis_index("mp")
    e = me // 2
    core = me % 2
    h = e % 4
    c = me // 8
    half = (me % 8) // 4
    sib = 2 * e + 1 - core

    def local(src, dst_, sem):
        cp = pltpu.make_async_copy(src, dst_, sem)
        cp.start()
        return cp

    def remote(src, dst_, ssem, rsem, dev):
        pltpu.make_async_remote_copy(
            src_ref=src, dst_ref=dst_, send_sem=ssem, recv_sem=rsem, device_id=dev, device_id_type=MESH
        ).start()

    def wait(ref, sem):
        pltpu.make_async_copy(ref, ref, sem).wait()

    cpx = local(x_hbm, x_v, in_sem.at[0])
    cpw = [local(w, w_v.at[j], in_sem.at[j + 1]) for j, w in enumerate((wq_hbm, wk_hbm, wv_hbm))]

    barrier = pltpu.get_barrier_semaphore()

    def greet(i, _):
        pl.semaphore_signal(barrier, inc=1, device_id=(lax.rem(me + i, NS), m), device_id_type=MESH)
        return 0

    lax.fori_loop(1, NS, greet, 0)

    def greet_far(i, _):
        far = lax.rem(m + 1 + i // NH, NM)
        pl.semaphore_signal(barrier, inc=1, device_id=(8 * c + 2 * (i % NH) + half, far), device_id_type=MESH)
        return 0

    lax.fori_loop(0, 3 * NH, greet_far, 0)
    for dm in range(1, NM):
        pl.semaphore_signal(barrier, inc=1, device_id=(me, lax.rem(m + dm, NM)), device_id_type=MESH)

    ids = ids_ref[...]
    member = ids == lax.broadcasted_iota(jnp.int32, (PM, B), 0)
    count = jnp.max(ids, axis=1, keepdims=True) + 1
    valid = lax.broadcasted_iota(jnp.int32, (PM, HD), 0) < count

    cpx.wait()
    x = x_v[...]
    scores = nt(pool_ref[...], x)
    a = jnp.concatenate([pool_softmax(scores[i : i + 1], member) for i in range(NH)], axis=0)
    a_hi, a_lo = split(a)
    xp = nn(jnp.concatenate([a_hi, a_lo], axis=0), x)
    xp_hi, xp_lo = split(xp[: NH * PM] + xp[NH * PM :])
    for i in range(NC):
        xps[i] = xp_hi[:, i * HD : (i + 1) * HD]
    xp2 = jnp.concatenate([xp_hi, xp_lo], axis=0)
    for j in range(3):
        cpw[j].wait()
        r = nn(xp2, w_v[j])
        r = r[: NH * PM] + r[NH * PM :]
        for i in range(NH):
            block = r[i * PM : (i + 1) * PM, i * HD : (i + 1) * HD]
            if j == 1:
                block = jnp.where(valid, block, MARK)
            qs[i, :, j * HD : (j + 1) * HD] = block.astype(BF16)
    g = g_ref[...].astype(F32)
    for i in range(NH):
        qs[i, :, 3 * HD :] = jnp.where(valid, g[:, i * HD : (i + 1) * HD], 0.0).astype(BF16)

    pl.semaphore_wait(barrier, NS - 1 + 3 * NH + 3)

    local(qs.at[h], rq.at[e, core], q_recv)
    local(xps.at[c, pl.ds(pl.multiple_of(h * PM, PM), PM)], rxp.at[e, core], x_recv)

    def send_q(i, _):
        to = lax.rem(e + i, NE)
        remote(qs.at[to % 4], rq.at[e, core], q_send, q_recv, (2 * to + core, m))
        return 0

    lax.fori_loop(1, NE, send_q, 0)

    def send_x(i, _):
        to = lax.rem(e + i, NE)
        src = xps.at[to // 4, pl.ds(pl.multiple_of((to % 4) * PM, PM), PM)]
        remote(src, rxp.at[e, core], x_send, x_recv, (2 * to + core, m))
        return 0

    lax.fori_loop(1, NE, send_x, 0)

    rp[m] = pool_ref[...]
    for dm in range(1, NM):
        remote(pool_ref, rp.at[m], pool_send.at[dm - 1], pool_recv.at[dm - 1], (me, lax.rem(m + dm, NM)))

    col = pl.ds(pl.multiple_of(h * HD, HD), HD)
    for j in range(3):
        wcat[:, j * HD : (j + 1) * HD] = w_v[j, :, col]

    wait(rq.at[:, core], q_recv)
    remote(rq.at[:, core], rq.at[:, core], f_send, f_recv, (sib, m))
    wait(rxp.at[:, core], x_recv)
    remote(rxp.at[:, core], rxp.at[:, core], fx_send, fx_recv, (sib, m))
    wait(rq.at[:, 1 - core], f_recv)

    k_raw = rq[:, :, :, HD : 2 * HD].reshape(SLOTS, HD).astype(F32)
    bad = k_raw > 0.5 * MARK
    kc[...] = jnp.where(bad, 0.0, k_raw).astype(BF16)
    bias[...] = jnp.where(bad, NEG, 0.0)

    def rows(lane, lo, hi):
        return rq[lo // 32 : hi // 32, :, :, lane * HD : (lane + 1) * HD].reshape(hi - lo, HD)

    for i in reversed(range(SLOTS // QB)):
        lo, n = i * QB, (i + 1) * QB
        q_i, g_i = rows(0, lo, n), rows(3, lo, n)
        t = nt(kc[:n], q_i) * (SCALE * LOG2E)
        b_n = bias[:n]
        t = t + jnp.concatenate([b_n] * (QB // HD), axis=1)
        seen = lax.broadcasted_iota(jnp.int32, (QB, QB), 0) <= lax.broadcasted_iota(jnp.int32, (QB, QB), 1)
        diag = jnp.where(seen, t[lo:], NEG)
        t = diag if i == 0 else jnp.concatenate([t[:lo], diag], axis=0)
        p = jnp.exp2(t - jnp.max(t, axis=0, keepdims=True))
        p = p * (1.0 / jnp.sum(p, axis=0, keepdims=True))
        pb = p.astype(BF16)
        pt[:n, lo:n] = pb
        dp = nt(rows(2, 0, n), g_i)
        delta = jnp.sum(pb.astype(F32) * dp, axis=0, keepdims=True)
        ds = (p * (dp - delta) * SCALE).astype(BF16)
        dst[:n, lo:n] = ds
        dqkv[lo:n, :HD] = tn(ds, kc[:n]).astype(BF16)
    for j in range(SLOTS // QB):
        lo = j * QB
        dqkv[lo : lo + QB, HD : 2 * HD] = nn(dst[lo : lo + QB, lo:], rows(0, lo, SLOTS)).astype(BF16)
        dqkv[lo : lo + QB, 2 * HD :] = nn(pt[lo : lo + QB, lo:], rows(3, lo, SLOTS)).astype(BF16)

    mine = dqkv[pl.ds(pl.multiple_of(8 * PM * c + 4 * PM * core, 4 * PM), 4 * PM), :]
    u = nt(mine, wcat[...]).astype(BF16)
    for t in range(4):
        us[t] = u[t * PM : (t + 1) * PM]
    owner0 = 8 * c + 4 * core

    for dm in range(NM):
        for t in range(4):
            if dm == 0:

                @pl.when(owner0 + t == me)
                def _():
                    local(us.at[t], ru.at[NH * m + h], u_recv.at[m])

                @pl.when(owner0 + t != me)
                def _():
                    remote(us.at[t], ru.at[NH * m + h], u_send, u_recv.at[m], (owner0 + t, m))
            else:
                remote(us.at[t], ru.at[NH * m + h], u_send, u_recv.at[m], (owner0 + t, lax.rem(m + dm, NM)))

    wait(rxp.at[:, 1 - core], fx_recv)
    gsend[...] = tn(rxp[...].reshape(SLOTS, HD), dqkv[...])
    for t in range(4):
        src = gsend.at[pl.ds(pl.multiple_of(4 * PM * core + t * PM, PM), PM)]

        @pl.when(owner0 + t == me)
        def _():
            local(src, rg.at[h], g_recv)

        @pl.when(owner0 + t != me)
        def _():
            remote(src, rg.at[h], g_send, g_recv, (owner0 + t, m))

    for dm in range(1, NM):
        wait(rp.at[0], pool_recv.at[dm - 1])
    rp_all = rp[...].reshape(NM * PM, DB)
    sc_all = nt(rp_all, x)
    for i in range(NM * NH):
        row = (i // NH) * PM + i % NH
        a_all[i * PM : (i + 1) * PM] = pool_softmax(sc_all[row : row + 1], member)

    wait(ru.at[pl.ds(0, NH)], u_recv.at[m])
    u_own = ru[pl.ds(pl.multiple_of(NH * m, NH), NH)].reshape(NH * PM, DB)

    def score_grad(uu, aa):
        ad = aa * nt(uu, x)
        s = jnp.sum(ad, axis=1, keepdims=True)
        d = ad - aa * s
        heads = aa.shape[0] // PM
        pad = jnp.zeros((PM - NH, B), F32)
        out = []
        for i in range(heads):
            out.append(jnp.sum(d[i * PM : (i + 1) * PM], axis=0, keepdims=True))
            if i % NH == NH - 1:
                out.append(pad)
        return jnp.concatenate(out, axis=0).astype(BF16)

    part = nn(score_grad(u_own, a), x)
    for i in range(NC):
        sc_send[i] = part[:8, i * HD : (i + 1) * HD]
    local(sc_send.at[c], rs.at[me], s_recv)

    def send_s(i, _):
        to = lax.rem(me + i, NS)
        remote(sc_send.at[to // 8], rs.at[me], s_send, s_recv, (to, m))
        return 0

    lax.fori_loop(1, NS, send_s, 0)

    for dm in range(1, NM):
        wait(ru.at[pl.ds(0, NH)], u_recv.at[lax.rem(m + dm, NM)])
    u_all = ru[...].reshape(NM * NH * PM, DB)
    aa = a_all[...]
    ds_all = score_grad(u_all, aa)
    left = jnp.concatenate([aa.astype(BF16), ds_all], axis=0)
    right = jnp.concatenate([u_all, rp_all], axis=0)
    dx_ref[...] = tn(left, right).astype(BF16)

    wait(rg, g_recv)
    for i in range(NH):
        for j, ref in enumerate((gq_ref, gk_ref, gv_ref)):
            ref[:, i * HD : (i + 1) * HD] = rg[i, :, j * HD : (j + 1) * HD]
    wait(rs, s_recv)
    tot = jnp.sum(rs[...], axis=0)
    tot = pltpu.roll(tot, lax.rem(HD - PM * (me % 8), HD), 1)
    gs_ref[...] = tot[:NH, :PM]

    for dm in range(1, NM):
        wait(pool_ref, pool_send.at[dm - 1])
    wait(rq.at[pl.ds(0, NE - 1), 0], q_send)
    wait(rxp.at[pl.ds(0, NE - 1), 0], x_send)
    wait(rq.at[:, 0], f_send)
    wait(rxp.at[:, 0], fx_send)
    own = half == core

    @pl.when(own)
    def _():
        wait(ru.at[pl.ds(0, 15)], u_send)
        wait(rg.at[pl.ds(0, 3)], g_send)

    @pl.when(jnp.logical_not(own))
    def _():
        wait(ru, u_send)
        wait(rg, g_send)

    wait(rs.at[pl.ds(0, NS - 1)], s_send)


def shards(byte_states, byte_patch, pool_score, w_query, w_key, w_value, out_grad):
    pool = jnp.pad(pool_score.T, ((0, PM - NH), (0, 0)))
    vmem = pl.BlockSpec(memory_space=pltpu.VMEM)
    hbm = pl.BlockSpec(memory_space=pl.ANY)
    dma = pltpu.SemaphoreType.DMA
    dx, gq, gk, gv, gs = pl.pallas_call(
        kernel,
        out_shape=(
            jax.ShapeDtypeStruct((B, DB), BF16),
            jax.ShapeDtypeStruct((PM, NH * HD), F32),
            jax.ShapeDtypeStruct((PM, NH * HD), F32),
            jax.ShapeDtypeStruct((PM, NH * HD), F32),
            jax.ShapeDtypeStruct((NH, PM), F32),
        ),
        in_specs=[hbm, vmem, vmem, hbm, hbm, hbm, vmem],
        out_specs=(vmem,) * 5,
        scratch_shapes=[
            pltpu.VMEM((B, DB), BF16),
            pltpu.VMEM((3, DB, NH * HD), BF16),
            pltpu.VMEM((DB, 3 * HD), BF16),
            pltpu.VMEM((NH, PM, 4 * HD), BF16),
            pltpu.VMEM((NC, NH * PM, HD), BF16),
            pltpu.VMEM((NE, 2, PM, 4 * HD), BF16),
            pltpu.VMEM((NE, 2, PM, HD), BF16),
            pltpu.VMEM((NM, PM, DB), BF16),
            pltpu.VMEM((SLOTS, HD), BF16),
            pltpu.VMEM((SLOTS, HD), F32),
            pltpu.VMEM((SLOTS, SLOTS), BF16),
            pltpu.VMEM((SLOTS, SLOTS), BF16),
            pltpu.VMEM((SLOTS, 3 * HD), BF16),
            pltpu.VMEM((4, PM, DB), BF16),
            pltpu.VMEM((NM * NH, PM, DB), BF16),
            pltpu.VMEM((HD, 3 * HD), F32),
            pltpu.VMEM((NH, PM, 3 * HD), F32),
            pltpu.VMEM((NC, 8, HD), F32),
            pltpu.VMEM((NS, 8, HD), F32),
            pltpu.VMEM((NM * NH * PM, B), F32),
            dma((4,)),
            dma((3,)), dma((3,)),
            dma, dma,
            dma, dma,
            dma, dma,
            dma, dma,
            dma, dma((NM,)),
            dma, dma,
            dma, dma,
        ],
        compiler_params=pltpu.CompilerParams(
            collective_id=0, has_side_effects=True, vmem_limit_bytes=48 * 1024 * 1024
        ),
    )(byte_states, byte_patch, pool, w_query, w_key, w_value, out_grad)
    return dx, gq, gk, gv, gs.T


def solution(mesh):
    return jax.shard_map(
        shards,
        mesh=mesh,
        in_specs=(
            P("seq", None),
            P("seq", None),
            P(None, "mp"),
            P(None, "mp"),
            P(None, "mp"),
            P(None, "mp"),
            P("seq", "mp"),
        ),
        out_specs=(P("seq", None), P("seq", "mp"), P("seq", "mp"), P("seq", "mp"), P("seq", "mp")),
        check_vma=False,
    )
```

```python
import jax
import jax.numpy as jnp
from jax import lax
from jax.experimental import pallas as pl
from jax.experimental.pallas import tpu as pltpu
from jax.sharding import PartitionSpec as P

HD = 128
PM = 16
NH = 4
NM = 4
NS = 64
NE = 32
EMIT = 8
NC = 8
B = 512
DB = 1024
SLOTS = 1024
QB = 256
SCALE = HD**-0.5
LOG2E = 1.4426950408889634
NEG = -1e30
MARK = 2.0**100
F32 = jnp.float32
BF16 = jnp.bfloat16
MESH = pl.DeviceIdType.MESH
OFFS = sorted(
    ((dx, dy, dz) for dz in range(2) for dy in range(4) for dx in range(4) if dx or dy or dz),
    key=lambda o: (-(min(o[0], 4 - o[0]) + min(o[1], 4 - o[1]) + o[2]), o),
)


def dot(a, b, dims):
    return lax.dot_general(a, b, (dims, ((), ())), preferred_element_type=F32)


def nn(a, b):
    return dot(a, b, ((1,), (0,)))


def nt(a, b):
    return dot(a, b, ((1,), (1,)))


def tn(a, b):
    return dot(a, b, ((0,), (0,)))


def split(a):
    hi = a.astype(BF16)
    return hi, (a - hi.astype(F32)).astype(BF16)


def pool_softmax(scores, member):
    t = jnp.where(member, scores, NEG)
    peak = jnp.max(t, axis=1, keepdims=True)
    expd = jnp.where(member, jnp.exp(t - peak), 0.0)
    total = jnp.sum(expd, axis=1, keepdims=True)
    return expd / jnp.maximum(total, 1e-30)


def kernel(
    x_hbm, ids_ref, pool_ref, wq_hbm, wk_hbm, wv_hbm, g_ref,
    dx_hbm, gw_hbm, gs_hbm,
    x_v, w_v, wcat, pool_v, qs, xps, rq, rxp, rp, kc, bias, pt, dst, dqkv, us, ru, gsend, rg, sc_send, rs, tot_send, rt, a_all, acc, dx_v, gw_v, gs_v,
    in_sem, pool_send, pool_recv, q_send, q_recv, x_send, x_recv, f_send, f_recv, fx_send, fx_recv,
    u_send, u_recv, v_send, g_send, g_recv, s_send, s_recv, t_send, t_recv, out_sem,
):
    me = lax.axis_index("seq")
    m = lax.axis_index("mp")
    e = me // 2
    core = me % 2
    h = e % 4
    c = me // 8
    half = (me % 8) // 4
    sib = 2 * e + 1 - core

    def local(src, dst_, sem):
        cp = pltpu.make_async_copy(src, dst_, sem)
        cp.start()
        return cp

    def remote(src, dst_, ssem, rsem, dev):
        pltpu.make_async_remote_copy(
            src_ref=src, dst_ref=dst_, send_sem=ssem, recv_sem=rsem, device_id=dev, device_id_type=MESH
        ).start()

    def wait(ref, sem):
        pltpu.make_async_copy(ref, ref, sem).wait()

    cpx = local(x_hbm, x_v, in_sem.at[0])
    cpw = [local(w, w_v.at[j], in_sem.at[j + 1]) for j, w in enumerate((wq_hbm, wk_hbm, wv_hbm))]

    def chip(off):
        z, y, xx = e // 16, (e // 4) % 4, e % 4
        return lax.rem(z + off[2], 2) * 16 + lax.rem(y + off[1], 4) * 4 + lax.rem(xx + off[0], 4)

    barrier = pltpu.get_barrier_semaphore()

    def greet(dev):
        pl.semaphore_signal(barrier, inc=1, device_id=dev, device_id_type=MESH)

    for off in OFFS:
        greet((2 * chip(off) + core, m))
    ahead, behind = lax.rem(m + 1, NM), lax.rem(m + 3, NM)
    for far in (ahead, behind):
        for i in range(NH):
            greet((8 * c + 2 * i + half, far))
    for dm in range(1, NM):
        greet((me, lax.rem(m + dm, NM)))
    for i in range(1, NH):
        greet((8 * c + 2 * lax.rem(h + i, NH) + 1 - core, m))
    greet((sib, m))

    ids = ids_ref[...]
    member = ids == lax.broadcasted_iota(jnp.int32, (PM, B), 0)
    count = jnp.max(ids, axis=1, keepdims=True) + 1
    valid = lax.broadcasted_iota(jnp.int32, (PM, HD), 0) < count

    cpx.wait()
    x = x_v[...]
    pool_v[...] = jnp.concatenate([pool_ref[...].astype(F32), jnp.zeros((PM - NH, DB), F32)], axis=0).astype(BF16)
    scores = nt(pool_v[...], x)
    a = jnp.concatenate([pool_softmax(scores[i : i + 1], member) for i in range(NH)], axis=0)
    a_hi, a_lo = split(a)
    xp = nn(jnp.concatenate([a_hi, a_lo], axis=0), x)
    xp_hi, xp_lo = split(xp[: NH * PM] + xp[NH * PM :])
    for i in range(NC):
        xps[i] = xp_hi[:, i * HD : (i + 1) * HD]
    xp2 = jnp.concatenate([xp_hi, xp_lo], axis=0)
    for j in range(3):
        cpw[j].wait()
        r = nn(xp2, w_v[j])
        r = r[: NH * PM] + r[NH * PM :]
        for i in range(NH):
            block = r[i * PM : (i + 1) * PM, i * HD : (i + 1) * HD]
            if j == 1:
                block = jnp.where(valid, block, MARK)
            qs[i, :, j * HD : (j + 1) * HD] = block.astype(BF16)
    g = g_ref[...].astype(F32)
    for i in range(NH):
        qs[i, :, 3 * HD :] = jnp.where(valid, g[:, i * HD : (i + 1) * HD], 0.0).astype(BF16)

    pl.semaphore_wait(barrier, len(OFFS) + 2 * NH + 3 + 3 + 1)

    local(qs.at[h], rq.at[e, core], q_recv)
    local(xps.at[c, pl.ds(pl.multiple_of(h * PM, PM), PM)], rxp.at[e, core], x_recv)

    for off in OFFS:
        to = chip(off)
        remote(qs.at[to % 4], rq.at[e, core], q_send, q_recv, (2 * to + core, m))

    def send_x(i, _):
        to = lax.rem(e + i, NE)
        src = xps.at[to // 4, pl.ds(pl.multiple_of((to % 4) * PM, PM), PM)]
        remote(src, rxp.at[e, core], x_send, x_recv, (2 * to + core, m))
        return 0

    lax.fori_loop(1, NE, send_x, 0)

    rp[m] = pool_v[...]
    for dm in range(1, NM):
        remote(pool_v, rp.at[m], pool_send.at[dm - 1], pool_recv.at[dm - 1], (me, lax.rem(m + dm, NM)))

    col = pl.ds(pl.multiple_of(h * HD, HD), HD)
    for j in range(3):
        wcat[:, j * HD : (j + 1) * HD] = w_v[j, :, col]

    wait(rq.at[:, core], q_recv)
    remote(rq.at[:, core], rq.at[:, core], f_send, f_recv, (sib, m))
    wait(rxp.at[:, core], x_recv)
    remote(rxp.at[:, core], rxp.at[:, core], fx_send, fx_recv, (sib, m))
    wait(rq.at[:, 1 - core], f_recv)

    k_raw = rq[:, :, :, HD : 2 * HD].reshape(SLOTS, HD).astype(F32)
    bad = k_raw > 0.5 * MARK
    kc[...] = jnp.where(bad, 0.0, k_raw).astype(BF16)
    bias[...] = jnp.where(bad, NEG, 0.0)

    def rows(lane, lo, hi):
        return rq[lo // 32 : hi // 32, :, :, lane * HD : (lane + 1) * HD].reshape(hi - lo, HD)

    for i in reversed(range(SLOTS // QB)):
        lo, n = i * QB, (i + 1) * QB
        q_i, g_i = rows(0, lo, n), rows(3, lo, n)
        t = nt(kc[:n], q_i) * (SCALE * LOG2E)
        b_n = bias[:n]
        t = t + jnp.concatenate([b_n] * (QB // HD), axis=1)
        seen = lax.broadcasted_iota(jnp.int32, (QB, QB), 0) <= lax.broadcasted_iota(jnp.int32, (QB, QB), 1)
        diag = jnp.where(seen, t[lo:], NEG)
        t = diag if i == 0 else jnp.concatenate([t[:lo], diag], axis=0)
        p = jnp.exp2(t - jnp.max(t, axis=0, keepdims=True))
        p = p * (1.0 / jnp.sum(p, axis=0, keepdims=True))
        pb = p.astype(BF16)
        pt[:n, lo:n] = pb
        dp = nt(rows(2, 0, n), g_i)
        delta = jnp.sum(pb.astype(F32) * dp, axis=0, keepdims=True)
        ds = (p * (dp - delta) * SCALE).astype(BF16)
        dst[:n, lo:n] = ds
        dqkv[lo:n, :HD] = tn(ds, kc[:n]).astype(BF16)
    for j in range(SLOTS // QB):
        lo = j * QB
        dqkv[lo : lo + QB, HD : 2 * HD] = nn(dst[lo : lo + QB, lo:], rows(0, lo, SLOTS)).astype(BF16)
        dqkv[lo : lo + QB, 2 * HD :] = nn(pt[lo : lo + QB, lo:], rows(3, lo, SLOTS)).astype(BF16)

    mine = dqkv[pl.ds(pl.multiple_of(8 * PM * c + 4 * PM * core, 4 * PM), 4 * PM), :]
    u = nt(mine, wcat[...]).astype(BF16)
    for t in range(4):
        us[t] = u[t * PM : (t + 1) * PM]
    owner0 = 8 * c + 4 * core

    def send_u(far):
        for t in range(4):
            remote(us.at[t], ru.at[NH * m + h], u_send, u_recv.at[m, h // 2], (owner0 + t, far))

    @pl.when(h < 2)
    def _():
        send_u(ahead)
        send_u(behind)

    @pl.when(h >= 2)
    def _():
        send_u(behind)
        send_u(ahead)

    for t in range(4):

        @pl.when(owner0 + t == me)
        def _():
            local(us.at[t], ru.at[NH * m + h], u_recv.at[m, h // 2])

        @pl.when(owner0 + t != me)
        def _():
            remote(us.at[t], ru.at[NH * m + h], u_send, u_recv.at[m, h // 2], (owner0 + t, m))

    wait(rxp.at[:, 1 - core], fx_recv)
    gsend[...] = tn(rxp[...].reshape(SLOTS, HD), dqkv[...])
    for t in range(4):
        src = gsend.at[pl.ds(pl.multiple_of(4 * PM * core + t * PM, PM), PM)]

        @pl.when(owner0 + t == me)
        def _():
            local(src, rg.at[h], g_recv)

        @pl.when(owner0 + t != me)
        def _():
            remote(src, rg.at[h], g_send, g_recv, (owner0 + t, m))

    for dm in range(1, NM):
        wait(rp.at[0], pool_recv.at[dm - 1])
    rp_all = rp[...].reshape(NM * PM, DB)
    sc_all = nt(rp_all, x)
    for i in range(NM * NH):
        row = (i // NH) * PM + i % NH
        a_all[i * PM : (i + 1) * PM] = pool_softmax(sc_all[row : row + 1], member)

    def heads(group, first, n):
        return pl.ds(NH * group + first, n)

    def arrived(group, part):
        wait(ru.at[pl.ds(0, 2)], u_recv.at[group, part])

    def group_of(group):
        u_g = ru[heads(group, 0, NH)].reshape(NH * PM, DB)
        a_g = a_all[pl.ds(pl.multiple_of(NH * PM * group, NH * PM), NH * PM), :]
        ad = a_g * nt(u_g, x)
        d = ad - a_g * jnp.sum(ad, axis=1, keepdims=True)
        rows_ = [jnp.sum(d[i * PM : (i + 1) * PM], axis=0, keepdims=True) for i in range(NH)]
        ds_g = jnp.concatenate(rows_ + [jnp.zeros((PM - NH, B), F32)], axis=0).astype(BF16)
        left = jnp.concatenate([a_g.astype(BF16), ds_g], axis=0)
        return ds_g, left, jnp.concatenate([u_g, rp[group]], axis=0)

    arrived(m, 0)
    arrived(m, 1)
    ds_own, left, right = group_of(m)
    part = nn(ds_own, x)
    for i in range(NC):
        sc_send[i] = part[:8, i * HD : (i + 1) * HD]
    local(sc_send.at[c], rs.at[c], s_recv)

    def send_s(i, _):
        to = lax.rem(c + i, NC)
        remote(sc_send.at[to], rs.at[c], s_send, s_recv, (8 * to + me % 8, m))
        return 0

    lax.fori_loop(1, NC, send_s, 0)

    opposite = lax.rem(m + 2, NM)
    arrived(behind, 0)
    remote(ru.at[heads(behind, 0, 2)], ru.at[heads(behind, 0, 2)], v_send.at[0], u_recv.at[behind, 0], (me, ahead))
    arrived(ahead, 1)
    remote(ru.at[heads(ahead, 2, 2)], ru.at[heads(ahead, 2, 2)], v_send.at[1], u_recv.at[ahead, 1], (me, behind))

    acc[...] = tn(left, right)

    wait(rs, s_recv)
    tot_send[...] = jnp.sum(rs[...], axis=0)
    local(tot_send, rt.at[me % 8], t_recv)

    def send_t(i, _):
        remote(tot_send, rt.at[me % 8], t_send, t_recv, (8 * c + lax.rem(me % 8 + i, 8), m))
        return 0

    lax.fori_loop(1, 8, send_t, 0)

    arrived(behind, 1)
    _, left, right = group_of(behind)
    acc[...] += tn(left, right)
    arrived(ahead, 0)
    _, left, right = group_of(ahead)
    acc[...] += tn(left, right)

    wait(rg, g_recv)
    for i in range(NH):
        for j in range(3):
            gw_v[j, :, i * HD : (i + 1) * HD] = rg[i, :, j * HD : (j + 1) * HD]
    out_w = local(gw_v, gw_hbm, out_sem.at[0])
    wait(rt, t_recv)
    tot = jnp.sum(rt[...], axis=0)
    tot = pltpu.roll(tot, lax.rem(HD - PM * (me % 8), HD), 1)
    gs_v[...] = tot[:NH, :PM]
    out_s = local(gs_v, gs_hbm, out_sem.at[1])

    arrived(opposite, 0)
    arrived(opposite, 1)
    _, left, right = group_of(opposite)
    out_x = []
    step = B // 4
    for i in range(4):
        at = pl.ds(i * step, step)
        dx_v[at, :] = (acc[at, :] + tn(left[:, i * step : (i + 1) * step], right)).astype(BF16)
        out_x.append(local(dx_v.at[at], dx_hbm.at[at], out_sem.at[2 + i]))

    for dm in range(1, NM):
        wait(pool_v, pool_send.at[dm - 1])
    wait(rq.at[pl.ds(0, NE - 1), 0], q_send)
    wait(rxp.at[pl.ds(0, NE - 1), 0], x_send)
    wait(rq.at[:, 0], f_send)
    wait(rxp.at[:, 0], fx_send)
    wait(ru.at[pl.ds(0, 2)], v_send.at[0])
    wait(ru.at[pl.ds(0, 2)], v_send.at[1])
    own = half == core

    @pl.when(own)
    def _():
        wait(ru.at[pl.ds(0, 11)], u_send)
        wait(rg.at[pl.ds(0, 3)], g_send)

    @pl.when(jnp.logical_not(own))
    def _():
        wait(ru.at[pl.ds(0, 12)], u_send)
        wait(rg, g_send)

    wait(rs.at[pl.ds(0, NC - 1)], s_send)
    wait(rt.at[pl.ds(0, 7)], t_send)
    for cp in [out_w, out_s] + out_x:
        cp.wait()


def emit(dx_in, gw_in, gs_in, dx_out, gq_out, gk_out, gv_out, gs_out, dx_v, gw_v, gs_v, in_sem, out_sem):
    step = B // EMIT
    ins, outs = [], []
    for i in range(EMIT):
        at = pl.ds(i * step, step)
        ins.append(pltpu.make_async_copy(dx_in.at[at], dx_v.at[at], in_sem.at[i]))
        outs.append(pltpu.make_async_copy(dx_v.at[at], dx_out.at[at], out_sem.at[i]))
    for i, ref in enumerate((gq_out, gk_out, gv_out)):
        ins.append(pltpu.make_async_copy(gw_in.at[i], gw_v.at[i], in_sem.at[EMIT + i]))
        outs.append(pltpu.make_async_copy(gw_v.at[i], ref, out_sem.at[EMIT + i]))
    ins.append(pltpu.make_async_copy(gs_in, gs_v, in_sem.at[EMIT + 3]))
    outs.append(pltpu.make_async_copy(gs_v, gs_out, out_sem.at[EMIT + 3]))
    for cp in ins:
        cp.start()
    for got, cp in zip(ins, outs):
        got.wait()
        cp.start()
    for cp in outs:
        cp.wait()


def shards(byte_states, byte_patch, pool_score, w_query, w_key, w_value, out_grad):
    pool = pool_score.T
    vmem = pl.BlockSpec(memory_space=pltpu.VMEM)
    anyspace = pl.BlockSpec(memory_space=pl.ANY)
    dma = pltpu.SemaphoreType.DMA
    x_shape = jax.ShapeDtypeStruct((B, DB), BF16)
    w_shape = jax.ShapeDtypeStruct((PM, NH * HD), F32)
    s_shape = jax.ShapeDtypeStruct((NH, PM), F32)
    made = pl.pallas_call(
        kernel,
        out_shape=(x_shape, jax.ShapeDtypeStruct((3, PM, NH * HD), F32), s_shape),
        in_specs=[anyspace, vmem, vmem, anyspace, anyspace, anyspace, vmem],
        out_specs=(anyspace,) * 3,
        scratch_shapes=[
            pltpu.VMEM((B, DB), BF16),
            pltpu.VMEM((3, DB, NH * HD), BF16),
            pltpu.VMEM((DB, 3 * HD), BF16),
            pltpu.VMEM((PM, DB), BF16),
            pltpu.VMEM((NH, PM, 4 * HD), BF16),
            pltpu.VMEM((NC, NH * PM, HD), BF16),
            pltpu.VMEM((NE, 2, PM, 4 * HD), BF16),
            pltpu.VMEM((NE, 2, PM, HD), BF16),
            pltpu.VMEM((NM, PM, DB), BF16),
            pltpu.VMEM((SLOTS, HD), BF16),
            pltpu.VMEM((SLOTS, HD), F32),
            pltpu.VMEM((SLOTS, SLOTS), BF16),
            pltpu.VMEM((SLOTS, SLOTS), BF16),
            pltpu.VMEM((SLOTS, 3 * HD), BF16),
            pltpu.VMEM((4, PM, DB), BF16),
            pltpu.VMEM((NM * NH, PM, DB), BF16),
            pltpu.VMEM((HD, 3 * HD), F32),
            pltpu.VMEM((NH, PM, 3 * HD), F32),
            pltpu.VMEM((NC, 8, HD), F32),
            pltpu.VMEM((NC, 8, HD), F32),
            pltpu.VMEM((8, HD), F32),
            pltpu.VMEM((8, 8, HD), F32),
            pltpu.VMEM((NM * NH * PM, B), F32),
            pltpu.VMEM((B, DB), F32),
            pltpu.VMEM((B, DB), BF16),
            pltpu.VMEM((3, PM, NH * HD), F32),
            pltpu.VMEM((NH, PM), F32),
            dma((4,)),
            dma((3,)), dma((3,)),
            dma, dma,
            dma, dma,
            dma, dma,
            dma, dma,
            dma, dma((NM, 2)),
            dma((2,)),
            dma, dma,
            dma, dma,
            dma, dma,
            dma((6,)),
        ],
        compiler_params=pltpu.CompilerParams(
            collective_id=0, has_side_effects=True, vmem_limit_bytes=61 * 1024 * 1024
        ),
    )(byte_states, byte_patch, pool, w_query, w_key, w_value, out_grad)
    dx, gq, gk, gv, gs = pl.pallas_call(
        emit,
        out_shape=(x_shape, w_shape, w_shape, w_shape, s_shape),
        in_specs=[anyspace] * 3,
        out_specs=(anyspace,) * 5,
        scratch_shapes=[
            pltpu.VMEM((B, DB), BF16),
            pltpu.VMEM((3, PM, NH * HD), F32),
            pltpu.VMEM((NH, PM), F32),
            dma((EMIT + 4,)),
            dma((EMIT + 4,)),
        ],
        compiler_params=pltpu.CompilerParams(vmem_limit_bytes=61 * 1024 * 1024),
    )(*made)
    return dx, gq, gk, gv, gs.T


def solution(mesh):
    return jax.shard_map(
        shards,
        mesh=mesh,
        in_specs=(
            P("seq", None),
            P("seq", None),
            P(None, "mp"),
            P(None, "mp"),
            P(None, "mp"),
            P(None, "mp"),
            P("seq", "mp"),
        ),
        out_specs=(P("seq", None), P("seq", "mp"), P("seq", "mp"), P("seq", "mp"), P("seq", "mp")),
        check_vma=False,
    )
```

```python
import jax
import jax.numpy as jnp
from jax import lax
from jax.experimental import pallas as pl
from jax.experimental.pallas import tpu as pltpu
from jax.sharding import PartitionSpec as P

HD = 128
PM = 16
NH = 4
NM = 4
NS = 64
NE = 32
EMIT = 8
NC = 8
B = 512
DB = 1024
SLOTS = 1024
QB = 256
SCALE = HD**-0.5
LOG2E = 1.4426950408889634
NEG = -1e30
MARK = 2.0**100
F32 = jnp.float32
BF16 = jnp.bfloat16
MESH = pl.DeviceIdType.MESH
OFFS = sorted(
    ((dx, dy, dz) for dz in range(2) for dy in range(4) for dx in range(4) if dx or dy or dz),
    key=lambda o: (-(min(o[0], 4 - o[0]) + min(o[1], 4 - o[1]) + o[2]), o),
)


def dot(a, b, dims):
    return lax.dot_general(a, b, (dims, ((), ())), preferred_element_type=F32)


def nn(a, b):
    return dot(a, b, ((1,), (0,)))


def nt(a, b):
    return dot(a, b, ((1,), (1,)))


def tn(a, b):
    return dot(a, b, ((0,), (0,)))


def split(a):
    hi = a.astype(BF16)
    return hi, (a - hi.astype(F32)).astype(BF16)


def pool_softmax(scores, member):
    t = jnp.where(member, scores, NEG)
    peak = jnp.max(t, axis=1, keepdims=True)
    expd = jnp.where(member, jnp.exp(t - peak), 0.0)
    total = jnp.sum(expd, axis=1, keepdims=True)
    return expd / jnp.maximum(total, 1e-30)


def kernel(
    x_hbm, ids_ref, pool_ref, wq_hbm, wk_hbm, wv_hbm, g_ref,
    dx_hbm, gw_hbm, gs_hbm,
    x_v, w_v, wcat, pool_v, qs, xps, rq, rxp, rp, kc, bias, pt, dst, dqkv, us, ru, gsend, rg, sc_send, rs, tot_send, rt, a_all, acc, dx_v, gw_v, gs_v,
    in_sem, pool_send, pool_recv, q_send, q_recv, x_send, x_recv, f_send, f_recv, fx_send, fx_recv,
    u_send, u_recv, v_send, g_send, g_recv, s_send, s_recv, t_send, t_recv, out_sem,
):
    me = lax.axis_index("seq")
    m = lax.axis_index("mp")
    e = me // 2
    core = me % 2
    h = e % 4
    c = me // 8
    half = (me % 8) // 4
    sib = 2 * e + 1 - core

    def local(src, dst_, sem):
        cp = pltpu.make_async_copy(src, dst_, sem)
        cp.start()
        return cp

    def remote(src, dst_, ssem, rsem, dev):
        pltpu.make_async_remote_copy(
            src_ref=src, dst_ref=dst_, send_sem=ssem, recv_sem=rsem, device_id=dev, device_id_type=MESH
        ).start()

    def wait(ref, sem):
        pltpu.make_async_copy(ref, ref, sem).wait()

    cpx = local(x_hbm, x_v, in_sem.at[0])
    cpw = [local(w, w_v.at[j], in_sem.at[j + 1]) for j, w in enumerate((wq_hbm, wk_hbm, wv_hbm))]

    def chip(off):
        z, y, xx = e // 16, (e // 4) % 4, e % 4
        return lax.rem(z + off[2], 2) * 16 + lax.rem(y + off[1], 4) * 4 + lax.rem(xx + off[0], 4)

    barrier = pltpu.get_barrier_semaphore()

    def greet(dev):
        pl.semaphore_signal(barrier, inc=1, device_id=dev, device_id_type=MESH)

    for off in OFFS:
        greet((2 * chip(off) + core, m))
    ahead, behind = lax.rem(m + 1, NM), lax.rem(m + 3, NM)
    for far in (ahead, behind):
        for i in range(NH):
            greet((8 * c + 2 * i + half, far))
    for dm in range(1, NM):
        greet((me, lax.rem(m + dm, NM)))
    for i in range(1, NH):
        greet((8 * c + 2 * lax.rem(h + i, NH) + 1 - core, m))
    greet((sib, m))

    ids = ids_ref[...]
    member = ids == lax.broadcasted_iota(jnp.int32, (PM, B), 0)
    count = jnp.max(ids, axis=1, keepdims=True) + 1
    valid = lax.broadcasted_iota(jnp.int32, (PM, HD), 0) < count

    cpx.wait()
    x = x_v[...]
    pool_v[...] = jnp.concatenate([pool_ref[...].astype(F32), jnp.zeros((PM - NH, DB), F32)], axis=0).astype(BF16)
    scores = nt(pool_v[...], x)
    a = jnp.concatenate([pool_softmax(scores[i : i + 1], member) for i in range(NH)], axis=0)
    a_hi, a_lo = split(a)
    xp = nn(jnp.concatenate([a_hi, a_lo], axis=0), x)
    xp_hi, xp_lo = split(xp[: NH * PM] + xp[NH * PM :])
    for i in range(NC):
        xps[i] = xp_hi[:, i * HD : (i + 1) * HD]
    xp2 = jnp.concatenate([xp_hi, xp_lo], axis=0)
    for j in range(3):
        cpw[j].wait()
        r = nn(xp2, w_v[j])
        r = r[: NH * PM] + r[NH * PM :]
        for i in range(NH):
            block = r[i * PM : (i + 1) * PM, i * HD : (i + 1) * HD]
            if j == 1:
                block = jnp.where(valid, block, MARK)
            qs[i, :, j * HD : (j + 1) * HD] = block.astype(BF16)
    g = g_ref[...].astype(F32)
    for i in range(NH):
        qs[i, :, 3 * HD :] = jnp.where(valid, g[:, i * HD : (i + 1) * HD], 0.0).astype(BF16)

    pl.semaphore_wait(barrier, len(OFFS) + 2 * NH + 3 + 3 + 1)

    local(qs.at[h], rq.at[e, core], q_recv)
    local(xps.at[c, pl.ds(pl.multiple_of(h * PM, PM), PM)], rxp.at[e, core], x_recv)

    for off in OFFS:
        to = chip(off)
        remote(qs.at[to % 4], rq.at[e, core], q_send, q_recv, (2 * to + core, m))

    def send_x(i, _):
        to = lax.rem(e + i, NE)
        src = xps.at[to // 4, pl.ds(pl.multiple_of((to % 4) * PM, PM), PM)]
        remote(src, rxp.at[e, core], x_send, x_recv, (2 * to + core, m))
        return 0

    lax.fori_loop(1, NE, send_x, 0)

    rp[m] = pool_v[...]
    for dm in range(1, NM):
        remote(pool_v, rp.at[m], pool_send.at[dm - 1], pool_recv.at[dm - 1], (me, lax.rem(m + dm, NM)))

    col = pl.ds(pl.multiple_of(h * HD, HD), HD)
    for j in range(3):
        wcat[j * HD : (j + 1) * HD, :] = w_v[j, :, col].T

    wait(rq.at[:, core], q_recv)
    remote(rq.at[:, core], rq.at[:, core], f_send, f_recv, (sib, m))
    wait(rq.at[:, 1 - core], f_recv)

    k_raw = rq[:, :, :, HD : 2 * HD].reshape(SLOTS, HD).astype(F32)
    bad = k_raw > 0.5 * MARK
    kc[...] = jnp.where(bad, 0.0, k_raw).astype(BF16)
    bias[...] = jnp.where(bad, NEG, 0.0)
    k_t = kc[...].T

    def rows(lane, lo, hi):
        return rq[lo // 32 : hi // 32, :, :, lane * HD : (lane + 1) * HD].reshape(hi - lo, HD)

    for i in reversed(range(SLOTS // QB)):
        lo, n = i * QB, (i + 1) * QB
        q_i, g_i = rows(0, lo, n), rows(3, lo, n)
        t = nt(kc[:n], q_i) * (SCALE * LOG2E)
        b_n = bias[:n]
        t = t + jnp.concatenate([b_n] * (QB // HD), axis=1)
        seen = lax.broadcasted_iota(jnp.int32, (QB, QB), 0) <= lax.broadcasted_iota(jnp.int32, (QB, QB), 1)
        diag = jnp.where(seen, t[lo:], NEG)
        t = diag if i == 0 else jnp.concatenate([t[:lo], diag], axis=0)
        p = jnp.exp2(t - jnp.max(t, axis=0, keepdims=True))
        p = p * (1.0 / jnp.sum(p, axis=0, keepdims=True))
        pb = p.astype(BF16)
        pt[:n, lo:n] = pb
        dp = nt(rows(2, 0, n), g_i)
        delta = jnp.sum(pb.astype(F32) * dp, axis=0, keepdims=True)
        ds = (p * (dp - delta) * SCALE).astype(BF16)
        dst[:n, lo:n] = ds
        dqkv[lo:n, :HD] = nn(k_t[:, :n], ds).T.astype(BF16)
    for j in range(SLOTS // QB):
        lo = j * QB
        dqkv[lo : lo + QB, HD : 2 * HD] = nn(dst[lo : lo + QB, lo:], rows(0, lo, SLOTS)).astype(BF16)
        dqkv[lo : lo + QB, 2 * HD :] = nn(pt[lo : lo + QB, lo:], rows(3, lo, SLOTS)).astype(BF16)

    wait(rxp.at[:, core], x_recv)
    remote(rxp.at[:, core], rxp.at[:, core], fx_send, fx_recv, (sib, m))
    mine = dqkv[pl.ds(pl.multiple_of(8 * PM * c + 4 * PM * core, 4 * PM), 4 * PM), :]
    u = nn(mine, wcat[...]).astype(BF16)
    for t in range(4):
        us[t] = u[t * PM : (t + 1) * PM]
    owner0 = 8 * c + 4 * core

    def send_u(far):
        for t in range(4):
            remote(us.at[t], ru.at[NH * m + h], u_send, u_recv.at[m, h], (owner0 + t, far))

    for t in range(4):

        @pl.when(owner0 + t == me)
        def _():
            local(us.at[t], ru.at[NH * m + h], u_recv.at[m, h])

        @pl.when(owner0 + t != me)
        def _():
            remote(us.at[t], ru.at[NH * m + h], u_send, u_recv.at[m, h], (owner0 + t, m))

    @pl.when(h < 2)
    def _():
        send_u(ahead)
        send_u(behind)

    @pl.when(h >= 2)
    def _():
        send_u(behind)
        send_u(ahead)

    for dm in range(1, NM):
        wait(rp.at[0], pool_recv.at[dm - 1])
    sc_all = nt(rp[...].reshape(NM * PM, DB), x)
    for i in range(NM * NH):
        row = (i // NH) * PM + i % NH
        a_all[i * PM : (i + 1) * PM] = pool_softmax(sc_all[row : row + 1], member)

    def arrived(group, first, n):
        for i in range(first, first + n):
            wait(ru.at[0], u_recv.at[group, i])

    def group_of(group):
        u_g = ru[pl.ds(NH * group, NH)].reshape(NH * PM, DB)
        a_g = a_all[pl.ds(pl.multiple_of(NH * PM * group, NH * PM), NH * PM), :]
        ad = a_g * nt(u_g, x)
        d = ad - a_g * jnp.sum(ad, axis=1, keepdims=True)
        rows_ = [jnp.sum(d[i * PM : (i + 1) * PM], axis=0, keepdims=True) for i in range(NH)]
        ds_g = jnp.concatenate(rows_ + [jnp.zeros((PM - NH, B), F32)], axis=0).astype(BF16)
        left = jnp.concatenate([a_g.astype(BF16), ds_g], axis=0)
        return ds_g, left, jnp.concatenate([u_g, rp[group]], axis=0)

    arrived(m, 0, NH)
    ds_own, left, right = group_of(m)
    part = nn(ds_own, x)
    for i in range(NC):
        sc_send[i] = part[:8, i * HD : (i + 1) * HD]
    local(sc_send.at[c], rs.at[c], s_recv)

    def send_s(i, _):
        to = lax.rem(c + i, NC)
        remote(sc_send.at[to], rs.at[c], s_send, s_recv, (8 * to + me % 8, m))
        return 0

    lax.fori_loop(1, NC, send_s, 0)

    opposite = lax.rem(m + 2, NM)
    for i in range(2):
        for n, (group, to, head) in enumerate(((behind, ahead, i), (ahead, behind, 2 + i))):
            arrived(group, head, 1)
            block = ru.at[NH * group + head]
            remote(block, block, v_send.at[n, i], u_recv.at[group, head], (me, to))

    wait(rxp.at[:, 1 - core], fx_recv)
    gsend[...] = tn(rxp[...].reshape(SLOTS, HD), dqkv[...])
    for t in range(4):
        src = gsend.at[pl.ds(pl.multiple_of(4 * PM * core + t * PM, PM), PM)]

        @pl.when(owner0 + t == me)
        def _():
            local(src, rg.at[h], g_recv)

        @pl.when(owner0 + t != me)
        def _():
            remote(src, rg.at[h], g_send, g_recv, (owner0 + t, m))

    acc[...] = tn(left, right)

    wait(rs, s_recv)
    tot_send[...] = jnp.sum(rs[...], axis=0)
    local(tot_send, rt.at[me % 8], t_recv)

    def send_t(i, _):
        remote(tot_send, rt.at[me % 8], t_send, t_recv, (8 * c + lax.rem(me % 8 + i, 8), m))
        return 0

    lax.fori_loop(1, 8, send_t, 0)

    arrived(behind, 2, 2)
    _, left, right = group_of(behind)
    acc[...] += tn(left, right)
    arrived(ahead, 0, 2)
    _, left, right = group_of(ahead)
    acc[...] += tn(left, right)

    wait(rg, g_recv)
    for i in range(NH):
        for j in range(3):
            gw_v[j, :, i * HD : (i + 1) * HD] = rg[i, :, j * HD : (j + 1) * HD]
    out_w = local(gw_v, gw_hbm, out_sem.at[0])
    wait(rt, t_recv)
    tot = jnp.sum(rt[...], axis=0)
    tot = pltpu.roll(tot, lax.rem(HD - PM * (me % 8), HD), 1)
    gs_v[...] = tot[:NH, :PM]
    out_s = local(gs_v, gs_hbm, out_sem.at[1])

    arrived(opposite, 0, NH)
    _, left, right = group_of(opposite)
    out_x = []
    step = B // 4
    for i in range(4):
        at = pl.ds(i * step, step)
        dx_v[at, :] = (acc[at, :] + tn(left[:, i * step : (i + 1) * step], right)).astype(BF16)
        out_x.append(local(dx_v.at[at], dx_hbm.at[at], out_sem.at[2 + i]))

    for dm in range(1, NM):
        wait(pool_v, pool_send.at[dm - 1])
    wait(rq.at[pl.ds(0, NE - 1), 0], q_send)
    wait(rxp.at[pl.ds(0, NE - 1), 0], x_send)
    wait(rq.at[:, 0], f_send)
    wait(rxp.at[:, 0], fx_send)
    for n in range(2):
        for i in range(2):
            wait(ru.at[0], v_send.at[n, i])
    own = half == core

    @pl.when(own)
    def _():
        wait(ru.at[pl.ds(0, 11)], u_send)
        wait(rg.at[pl.ds(0, 3)], g_send)

    @pl.when(jnp.logical_not(own))
    def _():
        wait(ru.at[pl.ds(0, 12)], u_send)
        wait(rg, g_send)

    wait(rs.at[pl.ds(0, NC - 1)], s_send)
    wait(rt.at[pl.ds(0, 7)], t_send)
    for cp in [out_w, out_s] + out_x:
        cp.wait()


def emit(dx_in, gw_in, gs_in, dx_out, gq_out, gk_out, gv_out, gs_out, dx_v, gw_v, gs_v, in_sem, out_sem):
    step = B // EMIT
    ins, outs = [], []
    for i in range(EMIT):
        at = pl.ds(i * step, step)
        ins.append(pltpu.make_async_copy(dx_in.at[at], dx_v.at[at], in_sem.at[i]))
        outs.append(pltpu.make_async_copy(dx_v.at[at], dx_out.at[at], out_sem.at[i]))
    for i, ref in enumerate((gq_out, gk_out, gv_out)):
        ins.append(pltpu.make_async_copy(gw_in.at[i], gw_v.at[i], in_sem.at[EMIT + i]))
        outs.append(pltpu.make_async_copy(gw_v.at[i], ref, out_sem.at[EMIT + i]))
    ins.append(pltpu.make_async_copy(gs_in, gs_v, in_sem.at[EMIT + 3]))
    outs.append(pltpu.make_async_copy(gs_v, gs_out, out_sem.at[EMIT + 3]))
    for cp in ins:
        cp.start()
    for got, cp in zip(ins, outs):
        got.wait()
        cp.start()
    for cp in outs:
        cp.wait()


def shards(byte_states, byte_patch, pool_score, w_query, w_key, w_value, out_grad):
    pool = pool_score.T
    vmem = pl.BlockSpec(memory_space=pltpu.VMEM)
    anyspace = pl.BlockSpec(memory_space=pl.ANY)
    dma = pltpu.SemaphoreType.DMA
    x_shape = jax.ShapeDtypeStruct((B, DB), BF16)
    w_shape = jax.ShapeDtypeStruct((PM, NH * HD), F32)
    s_shape = jax.ShapeDtypeStruct((NH, PM), F32)
    made = pl.pallas_call(
        kernel,
        out_shape=(x_shape, jax.ShapeDtypeStruct((3, PM, NH * HD), F32), s_shape),
        in_specs=[anyspace, vmem, vmem, anyspace, anyspace, anyspace, vmem],
        out_specs=(anyspace,) * 3,
        scratch_shapes=[
            pltpu.VMEM((B, DB), BF16),
            pltpu.VMEM((3, DB, NH * HD), BF16),
            pltpu.VMEM((3 * HD, DB), BF16),
            pltpu.VMEM((PM, DB), BF16),
            pltpu.VMEM((NH, PM, 4 * HD), BF16),
            pltpu.VMEM((NC, NH * PM, HD), BF16),
            pltpu.VMEM((NE, 2, PM, 4 * HD), BF16),
            pltpu.VMEM((NE, 2, PM, HD), BF16),
            pltpu.VMEM((NM, PM, DB), BF16),
            pltpu.VMEM((SLOTS, HD), BF16),
            pltpu.VMEM((SLOTS, HD), F32),
            pltpu.VMEM((SLOTS, SLOTS), BF16),
            pltpu.VMEM((SLOTS, SLOTS), BF16),
            pltpu.VMEM((SLOTS, 3 * HD), BF16),
            pltpu.VMEM((4, PM, DB), BF16),
            pltpu.VMEM((NM * NH, PM, DB), BF16),
            pltpu.VMEM((HD, 3 * HD), F32),
            pltpu.VMEM((NH, PM, 3 * HD), F32),
            pltpu.VMEM((NC, 8, HD), F32),
            pltpu.VMEM((NC, 8, HD), F32),
            pltpu.VMEM((8, HD), F32),
            pltpu.VMEM((8, 8, HD), F32),
            pltpu.VMEM((NM * NH * PM, B), F32),
            pltpu.VMEM((B, DB), F32),
            pltpu.VMEM((B, DB), BF16),
            pltpu.VMEM((3, PM, NH * HD), F32),
            pltpu.VMEM((NH, PM), F32),
            dma((4,)),
            dma((3,)), dma((3,)),
            dma, dma,
            dma, dma,
            dma, dma,
            dma, dma,
            dma, dma((NM, NH)),
            dma((2, 2)),
            dma, dma,
            dma, dma,
            dma, dma,
            dma((6,)),
        ],
        compiler_params=pltpu.CompilerParams(
            collective_id=0, has_side_effects=True, vmem_limit_bytes=61 * 1024 * 1024
        ),
    )(byte_states, byte_patch, pool, w_query, w_key, w_value, out_grad)
    dx, gq, gk, gv, gs = pl.pallas_call(
        emit,
        out_shape=(x_shape, w_shape, w_shape, w_shape, s_shape),
        in_specs=[anyspace] * 3,
        out_specs=(anyspace,) * 5,
        scratch_shapes=[
            pltpu.VMEM((B, DB), BF16),
            pltpu.VMEM((3, PM, NH * HD), F32),
            pltpu.VMEM((NH, PM), F32),
            dma((EMIT + 4,)),
            dma((EMIT + 4,)),
        ],
        compiler_params=pltpu.CompilerParams(vmem_limit_bytes=61 * 1024 * 1024),
    )(*made)
    return dx, gq, gk, gv, gs.T


def solution(mesh):
    return jax.shard_map(
        shards,
        mesh=mesh,
        in_specs=(
            P("seq", None),
            P("seq", None),
            P(None, "mp"),
            P(None, "mp"),
            P(None, "mp"),
            P(None, "mp"),
            P("seq", "mp"),
        ),
        out_specs=(P("seq", None), P("seq", "mp"), P("seq", "mp"), P("seq", "mp"), P("seq", "mp")),
        check_vma=False,
    )
```

```python
import jax
import jax.numpy as jnp
from jax import lax
from jax.experimental import pallas as pl
from jax.experimental.pallas import tpu as pltpu
from jax.sharding import PartitionSpec as P

HD = 128
PM = 16
NH = 4
NM = 4
NS = 64
NE = 32
EMIT = 4
NC = 8
B = 512
DB = 1024
SLOTS = 1024
QB = 256
SCALE = HD**-0.5
LOG2E = 1.4426950408889634
NEG = -1e30
MARK = 2.0**100
F32 = jnp.float32
BF16 = jnp.bfloat16
MESH = pl.DeviceIdType.MESH
OFFS = sorted(
    ((dx, dy, dz) for dz in range(2) for dy in range(4) for dx in range(4) if dx or dy or dz),
    key=lambda o: (-(min(o[0], 4 - o[0]) + min(o[1], 4 - o[1]) + o[2]), o),
)


def dot(a, b, dims):
    return lax.dot_general(a, b, (dims, ((), ())), preferred_element_type=F32)


def nn(a, b):
    return dot(a, b, ((1,), (0,)))


def nt(a, b):
    return dot(a, b, ((1,), (1,)))


def tn(a, b):
    return dot(a, b, ((0,), (0,)))


def split(a):
    hi = a.astype(BF16)
    return hi, (a - hi.astype(F32)).astype(BF16)


def pool_softmax(scores, member):
    t = jnp.where(member, scores, NEG)
    peak = jnp.max(t, axis=1, keepdims=True)
    expd = jnp.where(member, jnp.exp(t - peak), 0.0)
    total = jnp.sum(expd, axis=1, keepdims=True)
    return expd / jnp.maximum(total, 1e-30)


def kernel(
    x_hbm, ids_ref, pool_ref, wq_hbm, wk_hbm, wv_hbm, g_ref,
    dx_hbm, gw_hbm, gs_hbm,
    x_v, w_v, wcat, pool_v, qs, xps, rq, rxp, rp, kc, bias, pt, dst, kt_v, dc, dqkv, us, ru, gsend, rg, sc_send, rs, tot_send, rt, a_all, acc, dx_v, gw_v, gs_v,
    in_sem, pool_send, pool_recv, q_send, q_recv, x_send, x_recv, f_send, f_recv, fx_send, fx_recv,
    u_send, u_recv, v_send, g_send, g_recv, s_send, s_recv, t_send, t_recv, out_sem,
):
    me = lax.axis_index("seq")
    m = lax.axis_index("mp")
    e = me // 2
    core = me % 2
    h = e % 4
    c = me // 8
    half = (me % 8) // 4
    sib = 2 * e + 1 - core

    def local(src, dst_, sem):
        cp = pltpu.make_async_copy(src, dst_, sem)
        cp.start()
        return cp

    def remote(src, dst_, ssem, rsem, dev):
        pltpu.make_async_remote_copy(
            src_ref=src, dst_ref=dst_, send_sem=ssem, recv_sem=rsem, device_id=dev, device_id_type=MESH
        ).start()

    def wait(ref, sem):
        pltpu.make_async_copy(ref, ref, sem).wait()

    cpx = local(x_hbm, x_v, in_sem.at[0])
    cpw = [local(w, w_v.at[j], in_sem.at[j + 1]) for j, w in enumerate((wq_hbm, wk_hbm, wv_hbm))]

    def chip(off):
        z, y, xx = e // 16, (e // 4) % 4, e % 4
        return lax.rem(z + off[2], 2) * 16 + lax.rem(y + off[1], 4) * 4 + lax.rem(xx + off[0], 4)

    barrier = pltpu.get_barrier_semaphore()

    def greet(dev):
        pl.semaphore_signal(barrier, inc=1, device_id=dev, device_id_type=MESH)

    for off in OFFS:
        greet((2 * chip(off) + core, m))
    ahead, behind = lax.rem(m + 1, NM), lax.rem(m + 3, NM)
    for far in (ahead, behind):
        for i in range(NH):
            greet((8 * c + 2 * i + half, far))
    for dm in range(1, NM):
        greet((me, lax.rem(m + dm, NM)))
    for i in range(1, NH):
        greet((8 * c + 2 * lax.rem(h + i, NH) + 1 - core, m))
    greet((sib, m))

    ids = ids_ref[...]
    member = ids == lax.broadcasted_iota(jnp.int32, (PM, B), 0)
    count = jnp.max(ids, axis=1, keepdims=True) + 1
    valid = lax.broadcasted_iota(jnp.int32, (PM, HD), 0) < count

    cpx.wait()
    x = x_v[...]
    pool_v[...] = jnp.concatenate([pool_ref[...].astype(F32), jnp.zeros((PM - NH, DB), F32)], axis=0).astype(BF16)
    scores = nt(pool_v[...], x)
    a = jnp.concatenate([pool_softmax(scores[i : i + 1], member) for i in range(NH)], axis=0)
    a_hi, a_lo = split(a)
    xp = nn(jnp.concatenate([a_hi, a_lo], axis=0), x)
    xp_hi, xp_lo = split(xp[: NH * PM] + xp[NH * PM :])
    for i in range(NC):
        xps[i] = xp_hi[:, i * HD : (i + 1) * HD]
    xp2 = jnp.concatenate([xp_hi, xp_lo], axis=0)
    for j in range(3):
        cpw[j].wait()
        r = nn(xp2, w_v[j])
        r = r[: NH * PM] + r[NH * PM :]
        for i in range(NH):
            block = r[i * PM : (i + 1) * PM, i * HD : (i + 1) * HD]
            if j == 1:
                block = jnp.where(valid, block, MARK)
            qs[i, :, j * HD : (j + 1) * HD] = block.astype(BF16)
    g = g_ref[...].astype(F32)
    for i in range(NH):
        qs[i, :, 3 * HD :] = jnp.where(valid, g[:, i * HD : (i + 1) * HD], 0.0).astype(BF16)

    pl.semaphore_wait(barrier, len(OFFS) + 2 * NH + 3 + 3 + 1)

    local(qs.at[h], rq.at[e, core], q_recv)
    local(xps.at[c, pl.ds(pl.multiple_of(h * PM, PM), PM)], rxp.at[e, core], x_recv)

    for off in OFFS:
        to = chip(off)
        remote(qs.at[to % 4], rq.at[e, core], q_send, q_recv, (2 * to + core, m))

    rp[m] = pool_v[...]
    for dm in range(1, NM):
        remote(pool_v, rp.at[m], pool_send.at[dm - 1], pool_recv.at[dm - 1], (me, lax.rem(m + dm, NM)))

    col = pl.ds(pl.multiple_of(h * HD, HD), HD)
    for j in range(3):
        wcat[j * HD : (j + 1) * HD, :] = w_v[j, :, col].T

    for j in range(1, SLOTS // QB):
        blank = jnp.zeros((QB, j * QB), BF16)
        pt[j * QB : (j + 1) * QB, : j * QB] = blank
        dst[j * QB : (j + 1) * QB, : j * QB] = blank
    wait(rq.at[:, core], q_recv)
    remote(rq.at[:, core], rq.at[:, core], f_send, f_recv, (sib, m))
    def send_x(i, _):
        to = lax.rem(e + i, NE)
        src = xps.at[to // 4, pl.ds(pl.multiple_of((to % 4) * PM, PM), PM)]
        remote(src, rxp.at[e, core], x_send, x_recv, (2 * to + core, m))
        return 0

    lax.fori_loop(1, NE, send_x, 0)

    wait(rq.at[:, 1 - core], f_recv)

    k_raw = rq[:, :, :, HD : 2 * HD].reshape(SLOTS, HD).astype(F32)
    bad = k_raw > 0.5 * MARK
    kc[...] = jnp.where(bad, 0.0, k_raw).astype(BF16)
    bias[...] = jnp.where(bad, NEG, 0.0)
    kt_v[...] = kc[...].T

    def rows(lane, lo, hi):
        return rq[lo // 32 : hi // 32, :, :, lane * HD : (lane + 1) * HD].reshape(hi - lo, HD)

    for i in reversed(range(SLOTS // QB)):
        lo, n = i * QB, (i + 1) * QB
        q_i, g_i = rows(0, lo, n), rows(3, lo, n)
        t = nt(kc[:n], q_i) * (SCALE * LOG2E)
        b_n = bias[:n]
        t = t + jnp.concatenate([b_n] * (QB // HD), axis=1)
        seen = lax.broadcasted_iota(jnp.int32, (QB, QB), 0) <= lax.broadcasted_iota(jnp.int32, (QB, QB), 1)
        diag = jnp.where(seen, t[lo:], NEG)
        t = diag if i == 0 else jnp.concatenate([t[:lo], diag], axis=0)
        p = jnp.exp2(t - jnp.max(t, axis=0, keepdims=True))
        p = p * (1.0 / jnp.sum(p, axis=0, keepdims=True))
        pb = p.astype(BF16)
        pt[:n, lo:n] = pb
        dp = nt(rows(2, 0, n), g_i)
        delta = jnp.sum(pb.astype(F32) * dp, axis=0, keepdims=True)
        ds = (p * (dp - delta) * SCALE).astype(BF16)
        dst[:n, lo:n] = ds
    block = pl.ds(pl.multiple_of(HD * c, HD), HD)
    dc[:, :HD] = nn(kt_v[...], dst[:, block]).T.astype(BF16)
    dc[:, HD : 2 * HD] = nn(dst[block, :], rows(0, 0, SLOTS)).astype(BF16)
    dc[:, 2 * HD :] = nn(pt[block, :], rows(3, 0, SLOTS)).astype(BF16)
    mine = dc[pl.ds(pl.multiple_of(4 * PM * core, 4 * PM), 4 * PM), :]
    u = nn(mine, wcat[...]).astype(BF16)
    for t in range(4):
        us[t] = u[t * PM : (t + 1) * PM]
    owner0 = 8 * c + 4 * core

    def send_u(far):
        for t in range(4):
            remote(us.at[t], ru.at[NH * m + h], u_send, u_recv.at[m, h], (owner0 + t, far))

    for t in range(4):

        @pl.when(owner0 + t == me)
        def _():
            local(us.at[t], ru.at[NH * m + h], u_recv.at[m, h])

        @pl.when(owner0 + t != me)
        def _():
            remote(us.at[t], ru.at[NH * m + h], u_send, u_recv.at[m, h], (owner0 + t, m))

    @pl.when(h < 2)
    def _():
        send_u(ahead)
        send_u(behind)

    @pl.when(h >= 2)
    def _():
        send_u(behind)
        send_u(ahead)

    wait(rxp.at[:, core], x_recv)
    remote(rxp.at[:, core], rxp.at[:, core], fx_send, fx_recv, (sib, m))
    for dm in range(1, NM):
        wait(rp.at[0], pool_recv.at[dm - 1])
    sc_all = nt(rp[...].reshape(NM * PM, DB), x)
    for i in range(NM * NH):
        row = (i // NH) * PM + i % NH
        a_all[i * PM : (i + 1) * PM] = pool_softmax(sc_all[row : row + 1], member)

    def arrived(group, first, n):
        for i in range(first, first + n):
            wait(ru.at[0], u_recv.at[group, i])

    def group_of(group):
        u_g = ru[pl.ds(NH * group, NH)].reshape(NH * PM, DB)
        a_g = a_all[pl.ds(pl.multiple_of(NH * PM * group, NH * PM), NH * PM), :]
        ad = a_g * nt(u_g, x)
        d = ad - a_g * jnp.sum(ad, axis=1, keepdims=True)
        rows_ = [jnp.sum(d[i * PM : (i + 1) * PM], axis=0, keepdims=True) for i in range(NH)]
        ds_g = jnp.concatenate(rows_ + [jnp.zeros((PM - NH, B), F32)], axis=0).astype(BF16)
        left = jnp.concatenate([a_g.astype(BF16), ds_g], axis=0)
        return ds_g, left, jnp.concatenate([u_g, rp[group]], axis=0)

    arrived(m, 0, NH)
    ds_own, left, right = group_of(m)
    part = nn(ds_own, x)
    for i in range(NC):
        sc_send[i] = part[:8, i * HD : (i + 1) * HD]
    local(sc_send.at[c], rs.at[c], s_recv)

    def send_s(i, _):
        to = lax.rem(c + i, NC)
        remote(sc_send.at[to], rs.at[c], s_send, s_recv, (8 * to + me % 8, m))
        return 0

    lax.fori_loop(1, NC, send_s, 0)

    opposite = lax.rem(m + 2, NM)
    for i in range(2):
        for n, (group, to, head) in enumerate(((behind, ahead, i), (ahead, behind, 2 + i))):
            arrived(group, head, 1)
            block = ru.at[NH * group + head]
            remote(block, block, v_send.at[n, i], u_recv.at[group, head], (me, to))

    for i in range(SLOTS // QB):
        lo, n = i * QB, (i + 1) * QB
        dqkv[lo:n, :HD] = nn(kt_v[:, :n], dst[:n, lo:n]).T.astype(BF16)
    for j in range(SLOTS // QB):
        lo = j * QB
        dqkv[lo : lo + QB, HD : 2 * HD] = nn(dst[lo : lo + QB, lo:], rows(0, lo, SLOTS)).astype(BF16)
        dqkv[lo : lo + QB, 2 * HD :] = nn(pt[lo : lo + QB, lo:], rows(3, lo, SLOTS)).astype(BF16)

    wait(rxp.at[:, 1 - core], fx_recv)
    gsend[...] = tn(rxp[...].reshape(SLOTS, HD), dqkv[...])
    for t in range(4):
        src = gsend.at[pl.ds(pl.multiple_of(4 * PM * core + t * PM, PM), PM)]

        @pl.when(owner0 + t == me)
        def _():
            local(src, rg.at[h], g_recv)

        @pl.when(owner0 + t != me)
        def _():
            remote(src, rg.at[h], g_send, g_recv, (owner0 + t, m))

    acc[...] = tn(left, right)

    wait(rs, s_recv)
    tot_send[...] = jnp.sum(rs[...], axis=0)
    local(tot_send, rt.at[me % 8], t_recv)

    def send_t(i, _):
        remote(tot_send, rt.at[me % 8], t_send, t_recv, (8 * c + lax.rem(me % 8 + i, 8), m))
        return 0

    lax.fori_loop(1, 8, send_t, 0)

    arrived(behind, 2, 2)
    _, left, right = group_of(behind)
    acc[...] += tn(left, right)
    arrived(ahead, 0, 2)
    _, left, right = group_of(ahead)
    acc[...] += tn(left, right)

    wait(rg, g_recv)
    for i in range(NH):
        for j in range(3):
            gw_v[j, :, i * HD : (i + 1) * HD] = rg[i, :, j * HD : (j + 1) * HD]
    out_w = local(gw_v, gw_hbm, out_sem.at[0])
    wait(rt, t_recv)
    tot = jnp.sum(rt[...], axis=0)
    tot = pltpu.roll(tot, lax.rem(HD - PM * (me % 8), HD), 1)
    gs_v[...] = tot[:NH, :PM]
    out_s = local(gs_v, gs_hbm, out_sem.at[1])

    arrived(opposite, 0, NH)
    _, left, right = group_of(opposite)
    out_x = []
    step = B // 4
    for i in range(4):
        at = pl.ds(i * step, step)
        dx_v[at, :] = (acc[at, :] + tn(left[:, i * step : (i + 1) * step], right)).astype(BF16)
        out_x.append(local(dx_v.at[at], dx_hbm.at[at], out_sem.at[2 + i]))

    for dm in range(1, NM):
        wait(pool_v, pool_send.at[dm - 1])
    wait(rq.at[pl.ds(0, NE - 1), 0], q_send)
    wait(rxp.at[pl.ds(0, NE - 1), 0], x_send)
    wait(rq.at[:, 0], f_send)
    wait(rxp.at[:, 0], fx_send)
    for n in range(2):
        for i in range(2):
            wait(ru.at[0], v_send.at[n, i])
    own = half == core

    @pl.when(own)
    def _():
        wait(ru.at[pl.ds(0, 11)], u_send)
        wait(rg.at[pl.ds(0, 3)], g_send)

    @pl.when(jnp.logical_not(own))
    def _():
        wait(ru.at[pl.ds(0, 12)], u_send)
        wait(rg, g_send)

    wait(rs.at[pl.ds(0, NC - 1)], s_send)
    wait(rt.at[pl.ds(0, 7)], t_send)
    for cp in [out_w, out_s] + out_x:
        cp.wait()


def emit(dx_in, gw_in, gs_in, dx_out, gq_out, gk_out, gv_out, gs_out, dx_v, gw_v, gs_v, in_sem, out_sem):
    step = B // EMIT
    ins, outs = [], []
    for i in range(EMIT):
        at = pl.ds(i * step, step)
        ins.append(pltpu.make_async_copy(dx_in.at[at], dx_v.at[at], in_sem.at[i]))
        outs.append(pltpu.make_async_copy(dx_v.at[at], dx_out.at[at], out_sem.at[i]))
    for i, ref in enumerate((gq_out, gk_out, gv_out)):
        ins.append(pltpu.make_async_copy(gw_in.at[i], gw_v.at[i], in_sem.at[EMIT + i]))
        outs.append(pltpu.make_async_copy(gw_v.at[i], ref, out_sem.at[EMIT + i]))
    ins.append(pltpu.make_async_copy(gs_in, gs_v, in_sem.at[EMIT + 3]))
    outs.append(pltpu.make_async_copy(gs_v, gs_out, out_sem.at[EMIT + 3]))
    for cp in ins:
        cp.start()
    for got, cp in zip(ins, outs):
        got.wait()
        cp.start()
    for cp in outs:
        cp.wait()


def shards(byte_states, byte_patch, pool_score, w_query, w_key, w_value, out_grad):
    pool = pool_score.T
    vmem = pl.BlockSpec(memory_space=pltpu.VMEM)
    anyspace = pl.BlockSpec(memory_space=pl.ANY)
    dma = pltpu.SemaphoreType.DMA
    x_shape = jax.ShapeDtypeStruct((B, DB), BF16)
    w_shape = jax.ShapeDtypeStruct((PM, NH * HD), F32)
    s_shape = jax.ShapeDtypeStruct((NH, PM), F32)
    made = pl.pallas_call(
        kernel,
        out_shape=(x_shape, jax.ShapeDtypeStruct((3, PM, NH * HD), F32), s_shape),
        in_specs=[anyspace, vmem, vmem, anyspace, anyspace, anyspace, vmem],
        out_specs=(anyspace,) * 3,
        scratch_shapes=[
            pltpu.VMEM((B, DB), BF16),
            pltpu.VMEM((3, DB, NH * HD), BF16),
            pltpu.VMEM((3 * HD, DB), BF16),
            pltpu.VMEM((PM, DB), BF16),
            pltpu.VMEM((NH, PM, 4 * HD), BF16),
            pltpu.VMEM((NC, NH * PM, HD), BF16),
            pltpu.VMEM((NE, 2, PM, 4 * HD), BF16),
            pltpu.VMEM((NE, 2, PM, HD), BF16),
            pltpu.VMEM((NM, PM, DB), BF16),
            pltpu.VMEM((SLOTS, HD), BF16),
            pltpu.VMEM((SLOTS, HD), F32),
            pltpu.VMEM((SLOTS, SLOTS), BF16),
            pltpu.VMEM((SLOTS, SLOTS), BF16),
            pltpu.VMEM((HD, SLOTS), BF16),
            pltpu.VMEM((HD, 3 * HD), BF16),
            pltpu.VMEM((SLOTS, 3 * HD), BF16),
            pltpu.VMEM((4, PM, DB), BF16),
            pltpu.VMEM((NM * NH, PM, DB), BF16),
            pltpu.VMEM((HD, 3 * HD), F32),
            pltpu.VMEM((NH, PM, 3 * HD), F32),
            pltpu.VMEM((NC, 8, HD), F32),
            pltpu.VMEM((NC, 8, HD), F32),
            pltpu.VMEM((8, HD), F32),
            pltpu.VMEM((8, 8, HD), F32),
            pltpu.VMEM((NM * NH * PM, B), F32),
            pltpu.VMEM((B, DB), F32),
            pltpu.VMEM((B, DB), BF16),
            pltpu.VMEM((3, PM, NH * HD), F32),
            pltpu.VMEM((NH, PM), F32),
            dma((4,)),
            dma((3,)), dma((3,)),
            dma, dma,
            dma, dma,
            dma, dma,
            dma, dma,
            dma, dma((NM, NH)),
            dma((2, 2)),
            dma, dma,
            dma, dma,
            dma, dma,
            dma((6,)),
        ],
        compiler_params=pltpu.CompilerParams(
            collective_id=0, has_side_effects=True, vmem_limit_bytes=61 * 1024 * 1024
        ),
    )(byte_states, byte_patch, pool, w_query, w_key, w_value, out_grad)
    dx, gq, gk, gv, gs = pl.pallas_call(
        emit,
        out_shape=(x_shape, w_shape, w_shape, w_shape, s_shape),
        in_specs=[anyspace] * 3,
        out_specs=(anyspace,) * 5,
        scratch_shapes=[
            pltpu.VMEM((B, DB), BF16),
            pltpu.VMEM((3, PM, NH * HD), F32),
            pltpu.VMEM((NH, PM), F32),
            dma((EMIT + 4,)),
            dma((EMIT + 4,)),
        ],
        compiler_params=pltpu.CompilerParams(vmem_limit_bytes=61 * 1024 * 1024),
    )(*made)
    return dx, gq, gk, gv, gs.T


def solution(mesh):
    return jax.shard_map(
        shards,
        mesh=mesh,
        in_specs=(
            P("seq", None),
            P("seq", None),
            P(None, "mp"),
            P(None, "mp"),
            P(None, "mp"),
            P(None, "mp"),
            P("seq", "mp"),
        ),
        out_specs=(P("seq", None), P("seq", "mp"), P("seq", "mp"), P("seq", "mp"), P("seq", "mp")),
        check_vma=False,
    )
```

```python
import jax
import jax.numpy as jnp
from jax import lax
from jax.experimental import pallas as pl
from jax.experimental.pallas import tpu as pltpu
from jax.sharding import PartitionSpec as P

HD = 128
PM = 16
NH = 4
NM = 4
NS = 64
NE = 32
EMIT = 4
NC = 8
B = 512
DB = 1024
SLOTS = 1024
QB = 256
SCALE = HD**-0.5
LOG2E = 1.4426950408889634
NEG = -1e30
MARK = 2.0**100
F32 = jnp.float32
BF16 = jnp.bfloat16
MESH = pl.DeviceIdType.MESH
OFFS = sorted(
    ((dx, dy, dz) for dz in range(2) for dy in range(4) for dx in range(4) if dx or dy or dz),
    key=lambda o: (-(min(o[0], 4 - o[0]) + min(o[1], 4 - o[1]) + o[2]), o),
)


def dot(a, b, dims):
    return lax.dot_general(a, b, (dims, ((), ())), preferred_element_type=F32)


def nn(a, b):
    return dot(a, b, ((1,), (0,)))


def nt(a, b):
    return dot(a, b, ((1,), (1,)))


def tn(a, b):
    return dot(a, b, ((0,), (0,)))


def split(a):
    hi = a.astype(BF16)
    return hi, (a - hi.astype(F32)).astype(BF16)


def pool_softmax(scores, member):
    t = jnp.where(member, scores, NEG)
    peak = jnp.max(t, axis=1, keepdims=True)
    expd = jnp.where(member, jnp.exp(t - peak), 0.0)
    total = jnp.sum(expd, axis=1, keepdims=True)
    return expd / jnp.maximum(total, 1e-30)


def kernel(
    x_hbm, ids_ref, pool_ref, wq_hbm, wk_hbm, wv_hbm, g_ref,
    dx_hbm, gw_hbm, gs_hbm,
    x_v, w_v, wcat, pool_v, qs, xps, rq, rxp, rp, kc, bias, pt, dst, kt_v, dc, dqkv, us, ru, gsend, rg, sc_send, rs, tot_send, rt, a_all, acc, dx_v, gw_v, gs_v,
    in_sem, pool_send, pool_recv, q_send, q_recv, x_send, x_recv, f_send, f_recv, fx_send, fx_recv,
    u_send, u_recv, v_send, g_send, g_recv, s_send, s_recv, t_send, t_recv, out_sem,
):
    me = lax.axis_index("seq")
    m = lax.axis_index("mp")
    e = me // 2
    core = me % 2
    h = e % 4
    c = me // 8
    half = (me % 8) // 4
    sib = 2 * e + 1 - core

    def local(src, dst_, sem):
        cp = pltpu.make_async_copy(src, dst_, sem)
        cp.start()
        return cp

    def remote(src, dst_, ssem, rsem, dev):
        pltpu.make_async_remote_copy(
            src_ref=src, dst_ref=dst_, send_sem=ssem, recv_sem=rsem, device_id=dev, device_id_type=MESH
        ).start()

    def wait(ref, sem):
        pltpu.make_async_copy(ref, ref, sem).wait()

    cpx = local(x_hbm, x_v, in_sem.at[0])
    cpw = [local(w, w_v.at[j], in_sem.at[j + 1]) for j, w in enumerate((wq_hbm, wk_hbm, wv_hbm))]

    def chip(off):
        z, y, xx = e // 16, (e // 4) % 4, e % 4
        return lax.rem(z + off[2], 2) * 16 + lax.rem(y + off[1], 4) * 4 + lax.rem(xx + off[0], 4)

    barrier = pltpu.get_barrier_semaphore()

    def greet(dev):
        pl.semaphore_signal(barrier, inc=1, device_id=dev, device_id_type=MESH)

    for off in OFFS:
        greet((2 * chip(off) + core, m))
    ahead, behind = lax.rem(m + 1, NM), lax.rem(m + 3, NM)
    for far in (ahead, behind):
        for i in range(NH):
            greet((8 * c + 2 * i + half, far))
    for dm in range(1, NM):
        greet((me, lax.rem(m + dm, NM)))
    for i in range(1, NH):
        greet((8 * c + 2 * lax.rem(h + i, NH) + 1 - core, m))
    greet((sib, m))

    ids = ids_ref[...]
    member = ids == lax.broadcasted_iota(jnp.int32, (PM, B), 0)
    count = jnp.max(ids, axis=1, keepdims=True) + 1
    valid = lax.broadcasted_iota(jnp.int32, (PM, HD), 0) < count

    cpx.wait()
    x = x_v[...]
    pool_v[...] = jnp.concatenate([pool_ref[...].astype(F32), jnp.zeros((PM - NH, DB), F32)], axis=0).astype(BF16)
    scores = nt(pool_v[...], x)
    a = jnp.concatenate([pool_softmax(scores[i : i + 1], member) for i in range(NH)], axis=0)
    a_hi, a_lo = split(a)
    xp = nn(jnp.concatenate([a_hi, a_lo], axis=0), x)
    xp_hi, xp_lo = split(xp[: NH * PM] + xp[NH * PM :])
    for i in range(NC):
        xps[i] = xp_hi[:, i * HD : (i + 1) * HD]
    xp2 = jnp.concatenate([xp_hi, xp_lo], axis=0)
    for j in range(3):
        cpw[j].wait()
        r = nn(xp2, w_v[j])
        r = r[: NH * PM] + r[NH * PM :]
        for i in range(NH):
            block = r[i * PM : (i + 1) * PM, i * HD : (i + 1) * HD]
            if j == 1:
                block = jnp.where(valid, block, MARK)
            qs[i, :, j * HD : (j + 1) * HD] = block.astype(BF16)
    g = g_ref[...].astype(F32)
    for i in range(NH):
        qs[i, :, 3 * HD :] = jnp.where(valid, g[:, i * HD : (i + 1) * HD], 0.0).astype(BF16)

    pl.semaphore_wait(barrier, len(OFFS) + 2 * NH + 3 + 3 + 1)

    local(qs.at[h], rq.at[e, core], q_recv)
    local(xps.at[c, pl.ds(pl.multiple_of(h * PM, PM), PM)], rxp.at[e, core], x_recv)

    for off in OFFS:
        to = chip(off)
        remote(qs.at[to % 4], rq.at[e, core], q_send, q_recv, (2 * to + core, m))

    rp[m] = pool_v[...]
    for dm in range(1, NM):
        remote(pool_v, rp.at[m], pool_send.at[dm - 1], pool_recv.at[dm - 1], (me, lax.rem(m + dm, NM)))

    col = pl.ds(pl.multiple_of(h * HD, HD), HD)
    for j in range(3):
        wcat[j * HD : (j + 1) * HD, :] = w_v[j, :, col].T

    for j in range(1, SLOTS // QB):
        blank = jnp.zeros((QB, j * QB), BF16)
        pt[j * QB : (j + 1) * QB, : j * QB] = blank
        dst[j * QB : (j + 1) * QB, : j * QB] = blank
    wait(rq.at[:, core], q_recv)
    remote(rq.at[:, core], rq.at[:, core], f_send, f_recv, (sib, m))
    wait(rq.at[:, 1 - core], f_recv)

    k_raw = rq[:, :, :, HD : 2 * HD].reshape(SLOTS, HD).astype(F32)
    bad = k_raw > 0.5 * MARK
    kc[...] = jnp.where(bad, 0.0, k_raw).astype(BF16)
    bias[...] = jnp.where(bad, NEG, 0.0)
    kt_v[...] = kc[...].T

    def rows(lane, lo, hi):
        return rq[lo // 32 : hi // 32, :, :, lane * HD : (lane + 1) * HD].reshape(hi - lo, HD)

    for i in reversed(range(SLOTS // QB)):
        lo, n = i * QB, (i + 1) * QB
        q_i, g_i = rows(0, lo, n), rows(3, lo, n)
        t = nt(kc[:n], q_i) * (SCALE * LOG2E)
        b_n = bias[:n]
        t = t + jnp.concatenate([b_n] * (QB // HD), axis=1)
        seen = lax.broadcasted_iota(jnp.int32, (QB, QB), 0) <= lax.broadcasted_iota(jnp.int32, (QB, QB), 1)
        diag = jnp.where(seen, t[lo:], NEG)
        t = diag if i == 0 else jnp.concatenate([t[:lo], diag], axis=0)
        p = jnp.exp2(t - jnp.max(t, axis=0, keepdims=True))
        p = p * (1.0 / jnp.sum(p, axis=0, keepdims=True))
        pb = p.astype(BF16)
        pt[:n, lo:n] = pb
        dp = nt(rows(2, 0, n), g_i)
        delta = jnp.sum(pb.astype(F32) * dp, axis=0, keepdims=True)
        ds = (p * (dp - delta) * SCALE).astype(BF16)
        dst[:n, lo:n] = ds
    block = pl.ds(pl.multiple_of(HD * c, HD), HD)
    dc[:, :HD] = nn(kt_v[...], dst[:, block]).T.astype(BF16)
    dc[:, HD : 2 * HD] = nn(dst[block, :], rows(0, 0, SLOTS)).astype(BF16)
    dc[:, 2 * HD :] = nn(pt[block, :], rows(3, 0, SLOTS)).astype(BF16)
    mine = dc[pl.ds(pl.multiple_of(4 * PM * core, 4 * PM), 4 * PM), :]
    u = nn(mine, wcat[...]).astype(BF16)
    for t in range(4):
        us[t] = u[t * PM : (t + 1) * PM]
    owner0 = 8 * c + 4 * core

    def send_u(far):
        for t in range(4):
            remote(us.at[t], ru.at[NH * m + h], u_send, u_recv.at[m, h], (owner0 + t, far))

    for t in range(4):

        @pl.when(owner0 + t == me)
        def _():
            local(us.at[t], ru.at[NH * m + h], u_recv.at[m, h])

        @pl.when(owner0 + t != me)
        def _():
            remote(us.at[t], ru.at[NH * m + h], u_send, u_recv.at[m, h], (owner0 + t, m))

    @pl.when(h < 2)
    def _():
        send_u(ahead)
        send_u(behind)

    @pl.when(h >= 2)
    def _():
        send_u(behind)
        send_u(ahead)

    def send_x(i, _):
        to = lax.rem(e + i, NE)
        src = xps.at[to // 4, pl.ds(pl.multiple_of((to % 4) * PM, PM), PM)]
        remote(src, rxp.at[e, core], x_send, x_recv, (2 * to + core, m))
        return 0

    lax.fori_loop(1, NE, send_x, 0)

    for dm in range(1, NM):
        wait(rp.at[0], pool_recv.at[dm - 1])
    sc_all = nt(rp[...].reshape(NM * PM, DB), x)
    for i in range(NM * NH):
        row = (i // NH) * PM + i % NH
        a_all[i * PM : (i + 1) * PM] = pool_softmax(sc_all[row : row + 1], member)

    def arrived(group, first, n):
        for i in range(first, first + n):
            wait(ru.at[0], u_recv.at[group, i])

    def group_of(group):
        u_g = ru[pl.ds(NH * group, NH)].reshape(NH * PM, DB)
        a_g = a_all[pl.ds(pl.multiple_of(NH * PM * group, NH * PM), NH * PM), :]
        ad = a_g * nt(u_g, x)
        d = ad - a_g * jnp.sum(ad, axis=1, keepdims=True)
        rows_ = [jnp.sum(d[i * PM : (i + 1) * PM], axis=0, keepdims=True) for i in range(NH)]
        ds_g = jnp.concatenate(rows_ + [jnp.zeros((PM - NH, B), F32)], axis=0).astype(BF16)
        left = jnp.concatenate([a_g.astype(BF16), ds_g], axis=0)
        return ds_g, left, jnp.concatenate([u_g, rp[group]], axis=0)

    arrived(m, 0, NH)
    ds_own, left, right = group_of(m)
    part = nn(ds_own, x)
    for i in range(NC):
        sc_send[i] = part[:8, i * HD : (i + 1) * HD]
    local(sc_send.at[c], rs.at[c], s_recv)

    def send_s(i, _):
        to = lax.rem(c + i, NC)
        remote(sc_send.at[to], rs.at[c], s_send, s_recv, (8 * to + me % 8, m))
        return 0

    lax.fori_loop(1, NC, send_s, 0)

    opposite = lax.rem(m + 2, NM)
    for i in range(2):
        for n, (group, to, head) in enumerate(((behind, ahead, i), (ahead, behind, 2 + i))):
            arrived(group, head, 1)
            block = ru.at[NH * group + head]
            remote(block, block, v_send.at[n, i], u_recv.at[group, head], (me, to))

    wait(rxp.at[:, core], x_recv)
    remote(rxp.at[:, core], rxp.at[:, core], fx_send, fx_recv, (sib, m))
    for i in range(SLOTS // QB):
        lo, n = i * QB, (i + 1) * QB
        dqkv[lo:n, :HD] = nn(kt_v[:, :n], dst[:n, lo:n]).T.astype(BF16)
    for j in range(SLOTS // QB):
        lo = j * QB
        dqkv[lo : lo + QB, HD : 2 * HD] = nn(dst[lo : lo + QB, lo:], rows(0, lo, SLOTS)).astype(BF16)
        dqkv[lo : lo + QB, 2 * HD :] = nn(pt[lo : lo + QB, lo:], rows(3, lo, SLOTS)).astype(BF16)

    wait(rxp.at[:, 1 - core], fx_recv)
    gsend[...] = tn(rxp[...].reshape(SLOTS, HD), dqkv[...])
    for t in range(4):
        src = gsend.at[pl.ds(pl.multiple_of(4 * PM * core + t * PM, PM), PM)]

        @pl.when(owner0 + t == me)
        def _():
            local(src, rg.at[h], g_recv)

        @pl.when(owner0 + t != me)
        def _():
            remote(src, rg.at[h], g_send, g_recv, (owner0 + t, m))

    acc[...] = tn(left, right)

    wait(rs, s_recv)
    tot_send[...] = jnp.sum(rs[...], axis=0)
    local(tot_send, rt.at[me % 8], t_recv)

    def send_t(i, _):
        remote(tot_send, rt.at[me % 8], t_send, t_recv, (8 * c + lax.rem(me % 8 + i, 8), m))
        return 0

    lax.fori_loop(1, 8, send_t, 0)

    arrived(behind, 2, 2)
    _, left, right = group_of(behind)
    acc[...] += tn(left, right)
    arrived(ahead, 0, 2)
    _, left, right = group_of(ahead)
    acc[...] += tn(left, right)

    wait(rg, g_recv)
    for i in range(NH):
        for j in range(3):
            gw_v[j, :, i * HD : (i + 1) * HD] = rg[i, :, j * HD : (j + 1) * HD]
    out_w = local(gw_v, gw_hbm, out_sem.at[0])
    wait(rt, t_recv)
    tot = jnp.sum(rt[...], axis=0)
    tot = pltpu.roll(tot, lax.rem(HD - PM * (me % 8), HD), 1)
    gs_v[...] = tot[:NH, :PM]
    out_s = local(gs_v, gs_hbm, out_sem.at[1])

    arrived(opposite, 0, NH)
    _, left, right = group_of(opposite)
    out_x = []
    step = B // 4
    for i in range(4):
        at = pl.ds(i * step, step)
        dx_v[at, :] = (acc[at, :] + tn(left[:, i * step : (i + 1) * step], right)).astype(BF16)
        out_x.append(local(dx_v.at[at], dx_hbm.at[at], out_sem.at[2 + i]))

    for dm in range(1, NM):
        wait(pool_v, pool_send.at[dm - 1])
    wait(rq.at[pl.ds(0, NE - 1), 0], q_send)
    wait(rxp.at[pl.ds(0, NE - 1), 0], x_send)
    wait(rq.at[:, 0], f_send)
    wait(rxp.at[:, 0], fx_send)
    for n in range(2):
        for i in range(2):
            wait(ru.at[0], v_send.at[n, i])
    own = half == core

    @pl.when(own)
    def _():
        wait(ru.at[pl.ds(0, 11)], u_send)
        wait(rg.at[pl.ds(0, 3)], g_send)

    @pl.when(jnp.logical_not(own))
    def _():
        wait(ru.at[pl.ds(0, 12)], u_send)
        wait(rg, g_send)

    wait(rs.at[pl.ds(0, NC - 1)], s_send)
    wait(rt.at[pl.ds(0, 7)], t_send)
    for cp in [out_w, out_s] + out_x:
        cp.wait()


def emit(dx_in, gw_in, gs_in, dx_out, gq_out, gk_out, gv_out, gs_out, dx_v, gw_v, gs_v, in_sem, out_sem):
    step = B // EMIT
    ins, outs = [], []
    for i in range(EMIT):
        at = pl.ds(i * step, step)
        ins.append(pltpu.make_async_copy(dx_in.at[at], dx_v.at[at], in_sem.at[i]))
        outs.append(pltpu.make_async_copy(dx_v.at[at], dx_out.at[at], out_sem.at[i]))
    for i, ref in enumerate((gq_out, gk_out, gv_out)):
        ins.append(pltpu.make_async_copy(gw_in.at[i], gw_v.at[i], in_sem.at[EMIT + i]))
        outs.append(pltpu.make_async_copy(gw_v.at[i], ref, out_sem.at[EMIT + i]))
    ins.append(pltpu.make_async_copy(gs_in, gs_v, in_sem.at[EMIT + 3]))
    outs.append(pltpu.make_async_copy(gs_v, gs_out, out_sem.at[EMIT + 3]))
    for cp in ins:
        cp.start()
    for got, cp in zip(ins, outs):
        got.wait()
        cp.start()
    for cp in outs:
        cp.wait()


def shards(byte_states, byte_patch, pool_score, w_query, w_key, w_value, out_grad):
    pool = pool_score.T
    vmem = pl.BlockSpec(memory_space=pltpu.VMEM)
    anyspace = pl.BlockSpec(memory_space=pl.ANY)
    dma = pltpu.SemaphoreType.DMA
    x_shape = jax.ShapeDtypeStruct((B, DB), BF16)
    w_shape = jax.ShapeDtypeStruct((PM, NH * HD), F32)
    s_shape = jax.ShapeDtypeStruct((NH, PM), F32)
    made = pl.pallas_call(
        kernel,
        out_shape=(x_shape, jax.ShapeDtypeStruct((3, PM, NH * HD), F32), s_shape),
        in_specs=[anyspace, vmem, vmem, anyspace, anyspace, anyspace, vmem],
        out_specs=(anyspace,) * 3,
        scratch_shapes=[
            pltpu.VMEM((B, DB), BF16),
            pltpu.VMEM((3, DB, NH * HD), BF16),
            pltpu.VMEM((3 * HD, DB), BF16),
            pltpu.VMEM((PM, DB), BF16),
            pltpu.VMEM((NH, PM, 4 * HD), BF16),
            pltpu.VMEM((NC, NH * PM, HD), BF16),
            pltpu.VMEM((NE, 2, PM, 4 * HD), BF16),
            pltpu.VMEM((NE, 2, PM, HD), BF16),
            pltpu.VMEM((NM, PM, DB), BF16),
            pltpu.VMEM((SLOTS, HD), BF16),
            pltpu.VMEM((SLOTS, HD), F32),
            pltpu.VMEM((SLOTS, SLOTS), BF16),
            pltpu.VMEM((SLOTS, SLOTS), BF16),
            pltpu.VMEM((HD, SLOTS), BF16),
            pltpu.VMEM((HD, 3 * HD), BF16),
            pltpu.VMEM((SLOTS, 3 * HD), BF16),
            pltpu.VMEM((4, PM, DB), BF16),
            pltpu.VMEM((NM * NH, PM, DB), BF16),
            pltpu.VMEM((HD, 3 * HD), F32),
            pltpu.VMEM((NH, PM, 3 * HD), F32),
            pltpu.VMEM((NC, 8, HD), F32),
            pltpu.VMEM((NC, 8, HD), F32),
            pltpu.VMEM((8, HD), F32),
            pltpu.VMEM((8, 8, HD), F32),
            pltpu.VMEM((NM * NH * PM, B), F32),
            pltpu.VMEM((B, DB), F32),
            pltpu.VMEM((B, DB), BF16),
            pltpu.VMEM((3, PM, NH * HD), F32),
            pltpu.VMEM((NH, PM), F32),
            dma((4,)),
            dma((3,)), dma((3,)),
            dma, dma,
            dma, dma,
            dma, dma,
            dma, dma,
            dma, dma((NM, NH)),
            dma((2, 2)),
            dma, dma,
            dma, dma,
            dma, dma,
            dma((6,)),
        ],
        compiler_params=pltpu.CompilerParams(
            collective_id=0, has_side_effects=True, vmem_limit_bytes=61 * 1024 * 1024
        ),
    )(byte_states, byte_patch, pool, w_query, w_key, w_value, out_grad)
    dx, gq, gk, gv, gs = pl.pallas_call(
        emit,
        out_shape=(x_shape, w_shape, w_shape, w_shape, s_shape),
        in_specs=[anyspace] * 3,
        out_specs=(anyspace,) * 5,
        scratch_shapes=[
            pltpu.VMEM((B, DB), BF16),
            pltpu.VMEM((3, PM, NH * HD), F32),
            pltpu.VMEM((NH, PM), F32),
            dma((EMIT + 4,)),
            dma((EMIT + 4,)),
        ],
        compiler_params=pltpu.CompilerParams(vmem_limit_bytes=61 * 1024 * 1024),
    )(*made)
    return dx, gq, gk, gv, gs.T


def solution(mesh):
    return jax.shard_map(
        shards,
        mesh=mesh,
        in_specs=(
            P("seq", None),
            P("seq", None),
            P(None, "mp"),
            P(None, "mp"),
            P(None, "mp"),
            P(None, "mp"),
            P("seq", "mp"),
        ),
        out_specs=(P("seq", None), P("seq", "mp"), P("seq", "mp"), P("seq", "mp"), P("seq", "mp")),
        check_vma=False,
    )
```
